32 devices in a mesh: parts: 2 (over y), gx: 4 (over x, core), yz: 4 (over z).
Axes of the slice: x: 2, y: 2, z: 4, core: 2. Of those that a mesh axis runs over, the one named last changes fastest.
Arguments:
- tokens: bfloat16 [128, 18432], P(('parts', 'gx', 'yz')), parts along dimension 0, may hold values from -1500 to 1500
- gain: float32 [18432], replicated, may hold values from 0.1 to 1.9
- w_qkv: bfloat16 [18432, 12800], P('gx', 'yz'), may hold values from -0.046875 to 0.046875
- w_out: bfloat16 [12288, 18432], P('yz', 'gx'), may hold values from -0.21875 to 0.21875
- cache_keys: bfloat16 [128, 1024, 256], P(('parts', 'gx', 'yz')), parts along dimension 0, may hold values from -600 to 600
- cache_values: bfloat16 [128, 1024, 256], P(('parts', 'gx', 'yz')), parts along dimension 0, may hold values from -6 to 6
- cache_lengths: int32 [128], P(('parts', 'gx', 'yz')), parts along dimension 0, may hold values from 2 to 1024, as said below
Outputs:
- branch: bfloat16 [4, 32, 18432], P(None, ('parts', 'yz'), 'gx'), parts along dimension 1
The draws below stay inside these ranges and needn't reach their ends.
There are 2 independent parts, one for each index of `parts`. The reference program is written for one: setup_inputs(seed, part) draws one part's arguments, and reference() takes and returns one part's arrays. A program takes and returns all parts, laid end to end along the dimension named above; an argument that names none is the same for every part. Nothing has to cross between parts.
Inputs may be any that keep to these rules, and one draw needn't show every extreme that they name: `cache_lengths`: filled slots of each sequence; some sequence uses all 1024 slots and some only 2.
All inputs are finite; a program needn't handle non-finite values.
Results may differ from the reference program's by a relative error of at most 0.012.
Values may be sent and summed in bfloat16 or wider, within the bound.
No kernel may reach another device: no remote copies, remote signals or barrier semaphores. Data moves between devices by JAX's collectives and lax.ppermute only.
A program may use at most 384 MiB of HBM per device.

```python
import math
import jax
import jax.numpy as jnp
from jax import lax

D = 18432
HEADS = 48
HEAD = 256
CACHE = 1024
QKV = 12800
SEQS = 64
GROUPS = 4
GROUP_ROWS = 16


def draw_tokens(key, part):
    key = jax.random.fold_in(key, 3)
    first, second, third = jax.random.split(key, 3)
    base = jnp.clip(jax.random.normal(first, (SEQS, D), jnp.float32), -6.0, 6.0)
    column_scale = jnp.exp(jax.random.uniform(second, (1, D), jnp.float32) * math.log(10.0))
    row_scale = jnp.exp(jax.random.uniform(third, (SEQS, 1), jnp.float32) * math.log(10.0))
    values = base * column_scale * row_scale
    return values.astype(jnp.bfloat16)


def draw_cache_keys(key, part):
    key = jax.random.fold_in(key, 7)
    base = 1.5 * jnp.clip(jax.random.normal(key, (SEQS, CACHE, HEAD), jnp.float32), -6.0, 6.0)
    values = base
    return values.astype(jnp.bfloat16)


def draw_cache_lengths(key, part):
    key = jax.random.fold_in(key, 5)
    lengths = jax.random.randint(key, (SEQS,), 2, CACHE + 1, jnp.int32)
    position = jnp.arange(SEQS, dtype=jnp.int32)
    lengths = jnp.where(position == 0, CACHE, lengths)
    return jnp.where(position == 1, 2, lengths).astype(jnp.int32)


def shard_levels(stream_key, shape, cuts, smallest, largest):
    def one(axis_at, shards_of):
        steps = jax.random.uniform(jax.random.fold_in(jax.random.fold_in(stream_key, 6), axis_at), (shards_of,), jnp.float32, smallest / len(cuts), largest / len(cuts))
        return jnp.repeat(jnp.exp(steps), shape[axis_at] // shards_of).reshape((-1,) + (1,) * (len(shape) - axis_at - 1))

    level = one(*cuts[0])
    for cut in cuts[1:]:
        level = level * one(*cut)
    return level


def noise(own_key, extent, scale, bound, pieces=(), held_as=jnp.bfloat16):
    array = jax.random.normal(own_key, extent, jnp.float32) * scale
    if len(pieces) > 0:
        array = shard_levels(own_key, extent, pieces, -0.22, 0.18) * array
    return jnp.clip(array, min=-bound, max=bound).astype(held_as)


def setup_inputs(seed: int = 0, part: int = 0) -> dict:
    arg_keys = jax.random.split(jax.random.key(seed), 8)
    part_splits = jax.random.split(jax.random.fold_in(arg_keys[7], part), 8)
    return {
        "tokens": draw_tokens(jax.random.fold_in(jax.random.fold_in(arg_keys[7], part), 71), part),
        "gain": jnp.clip(1.0 + 0.18 * jax.random.normal(arg_keys[1], (D,), jnp.float32), 0.1, 1.9),
        "w_qkv": noise(arg_keys[2], (D, QKV), D ** -0.5, 0.046875, ((0, 4), (1, 4))),
        "w_out": noise(arg_keys[3], (HEADS * HEAD, D), (HEADS * HEAD // 16) ** -0.5, 0.21875, ((0, 4), (1, 4))),
        "cache_keys": draw_cache_keys(jax.random.fold_in(jax.random.fold_in(arg_keys[7], part), 71), part),
        "cache_values": noise(part_splits[5], (SEQS, CACHE, HEAD), 1.0, 6.0, ((0, 16),)),
        "cache_lengths": draw_cache_lengths(jax.random.fold_in(jax.random.fold_in(arg_keys[7], part), 71), part),
    }


def attend_one(items):
    query, keys, values, length, key_new, value_new = items
    scale = 1.0 / jnp.sqrt(jnp.float32(HEAD))
    qf = query.astype(jnp.float32)
    scores = jnp.einsum('hd,td->ht', qf, keys.astype(jnp.float32)) * scale
    own = jnp.einsum('hd,d->h', qf, key_new.astype(jnp.float32)) * scale
    valid = jnp.arange(CACHE, dtype=jnp.int32)[None, :] < length
    masked = jnp.where(valid, scores, -jnp.inf)
    top = jnp.maximum(lax.optimization_barrier(jnp.max(masked, axis=1)), own)
    weights = jnp.where(valid, jnp.exp(masked - top[:, None]), 0.0)
    own_weight = jnp.exp(own - top)
    total = lax.optimization_barrier(jnp.sum(weights, axis=1)) + own_weight
    probs = (weights / total[:, None]).astype(jnp.bfloat16)
    own_prob = (own_weight / total).astype(jnp.bfloat16)
    mixed = jnp.einsum('ht,td->hd', probs.astype(jnp.float32), values.astype(jnp.float32))
    mixed = mixed + own_prob.astype(jnp.float32)[:, None] * value_new.astype(jnp.float32)[None, :]
    return mixed.astype(jnp.bfloat16).reshape(HEADS * HEAD)

def reference(tokens, gain, w_qkv, w_out, cache_keys, cache_values, cache_lengths):
    xf = tokens.astype(jnp.float32)
    mean = lax.optimization_barrier(jnp.mean(xf, axis=1, keepdims=True))
    centered = xf - mean
    variance = lax.optimization_barrier(jnp.mean(centered * centered, axis=1, keepdims=True))
    normed = (centered / jnp.sqrt(variance + 1e-05) * gain[None, :]).astype(jnp.bfloat16)
    qkv = jnp.dot(normed, w_qkv, preferred_element_type=jnp.float32).astype(jnp.bfloat16)
    width = HEADS * HEAD
    query = qkv[:, :width].reshape(SEQS, HEADS, HEAD)
    key_new = qkv[:, width:width + HEAD]
    value_new = qkv[:, width + HEAD:]
    attended = lax.map(attend_one, (query, cache_keys, cache_values, cache_lengths, key_new, value_new))
    branch = jnp.dot(attended, w_out, preferred_element_type=jnp.float32).astype(jnp.bfloat16)
    return branch.reshape(GROUPS, GROUP_ROWS, D)
```

```python
import functools

import jax
import jax.numpy as jnp
from jax import lax
from jax.experimental import pallas as pl
from jax.experimental.pallas import tpu as pltpu
from jax.sharding import PartitionSpec as P

VMEM = pl.BlockSpec(memory_space=pltpu.VMEM)
SMEM = pl.BlockSpec(memory_space=pltpu.SMEM)
ANY = pl.BlockSpec(memory_space=pl.ANY)
MIB = 1 << 20


def call(body, outs, in_specs, args, limit=8, scratch=(), flops=0, traffic=0):
    return pl.pallas_call(
        body,
        out_shape=outs,
        in_specs=in_specs,
        out_specs=jax.tree.map(lambda _: VMEM, outs),
        scratch_shapes=scratch,
        compiler_params=pltpu.CompilerParams(vmem_limit_bytes=limit * MIB),
        cost_estimate=pl.CostEstimate(flops=flops, bytes_accessed=traffic, transcendentals=0),
    )(*args)


def struct(shape, dtype=jnp.bfloat16):
    return jax.ShapeDtypeStruct(shape, dtype)


def exchange(pieces, axis):
    size = lax.axis_size(axis)
    return [pieces[0]] + [
        lax.ppermute(pieces[k], axis, [(i, i ^ k) for i in range(size)]) for k in range(1, size)
    ]


def norm_body(x_ref, gain_ref, *out_refs):
    block = out_refs[0].shape[1]
    me = lax.axis_index("gx")
    x = x_ref[...].astype(jnp.float32)
    mean = jnp.mean(x, axis=1, keepdims=True)
    centered = x - mean
    variance = jnp.mean(centered * centered, axis=1, keepdims=True)
    inverse = 1.0 / jnp.sqrt(variance + 1e-05)
    for k, out_ref in enumerate(out_refs):
        columns = pl.ds(pl.multiple_of((me ^ k) * block, 128), block)
        part = x_ref[:, columns].astype(jnp.float32) - mean
        out_ref[...] = (part * inverse * gain_ref[:, columns]).astype(jnp.bfloat16)


def load_body(w_ref, _, out_ref, sem):
    copy = pltpu.make_async_copy(w_ref, out_ref, sem)
    copy.start()
    copy.wait()


def load(w, after):
    w, after = lax.optimization_barrier((w, after))
    size = w.shape[0] * w.shape[1] * 2
    return pl.pallas_call(
        load_body,
        out_shape=pltpu.VMEM(w.shape, w.dtype),
        in_specs=[ANY, ANY],
        out_specs=VMEM,
        scratch_shapes=[pltpu.SemaphoreType.DMA],
        compiler_params=pltpu.CompilerParams(vmem_limit_bytes=MIB),
        cost_estimate=pl.CostEstimate(flops=0, bytes_accessed=2 * size, transcendentals=0),
    )(w, after)


def project_body(tile, n, *refs):
    pieces, w_ref, outs = refs[:n], refs[n], refs[n + 1 :]
    rows = jnp.concatenate([p[...] for p in pieces], axis=0)
    width = w_ref.shape[1]
    each = rows.shape[0] // (n * n)

    @pl.loop(0, width // tile)
    def _(i):
        columns = pl.ds(pl.multiple_of(i * tile, 128), tile)
        total = jnp.dot(rows, w_ref[:, columns], preferred_element_type=jnp.float32)
        for k, out in enumerate(outs):
            group = [
                total[(j * n + k) * each : (j * n + k + 1) * each] for j in range(n)
            ]
            out[:, columns] = jnp.concatenate(group, axis=0).astype(out.dtype)


def project(pieces, w, tile):
    n = len(pieces)
    rows, width = pieces[0].shape[0], w.shape[1]
    outs = [struct((rows, width), jnp.float32 if k == 0 else jnp.bfloat16) for k in range(n)]
    w = pltpu.with_memory_space_constraint(w, pltpu.VMEM)
    return call(
        functools.partial(project_body, tile, n),
        outs,
        [VMEM] * (n + 1),
        [*pieces, w],
        limit=12,
        flops=2 * n * rows * w.shape[0] * width,
        traffic=2 * w.shape[0] * width,
    )


def total_body(*refs):
    ins, outs = refs[: len(refs) // 2], refs[len(refs) // 2 :]
    total = ins[0][...]
    for r in ins[1:]:
        total = total + r[...].astype(jnp.float32)
    each = outs[0].shape[0]
    for j, out in enumerate(outs):
        out[...] = total[j * each : (j + 1) * each].astype(jnp.bfloat16)


def attend_body(blocks, heads, length_ref, *refs):
    pieces, (key_ref, value_ref) = refs[:blocks], refs[blocks : blocks + 2]
    outs = refs[blocks + 2 : 2 * blocks + 2]
    row_ref, query_ref, mixed_ref = refs[2 * blocks + 2 :]
    me = lax.axis_index("yz")
    part = pieces[0].shape[1]
    seqs, slots, head = key_ref.shape
    scale = 1.0 / jnp.sqrt(jnp.float32(head))
    for j, piece in enumerate(pieces):
        row_ref[:, pl.ds(pl.multiple_of((me ^ j) * part, 128), part)] = piece[...].astype(jnp.float32)
    for h in range(heads):
        query_ref[h] = row_ref[:, h * head : (h + 1) * head]
    slot = lax.broadcasted_iota(jnp.int32, (1, slots), 1)
    width = heads * head
    for s in range(seqs):
        query = query_ref[:, s, :]
        key_new = row_ref[s : s + 1, width : width + head]
        value_new = row_ref[s : s + 1, width + head : width + 2 * head]
        own = jnp.sum(query * key_new, axis=1, keepdims=True) * scale
        scores = lax.dot_general(
            query.astype(jnp.bfloat16),
            key_ref[s],
            (((1,), (1,)), ((), ())),
            preferred_element_type=jnp.float32,
        )
        masked = jnp.where(slot < length_ref[s], scores * scale, -jnp.inf)
        top = jnp.maximum(jnp.max(masked, axis=1, keepdims=True), own)
        weights = jnp.exp(masked - top)
        own_weight = jnp.exp(own - top)
        total = jnp.sum(weights, axis=1, keepdims=True) + own_weight
        probs = (weights / total).astype(jnp.bfloat16)
        own_prob = (own_weight / total).astype(jnp.bfloat16).astype(jnp.float32)
        mixed = jnp.dot(probs, value_ref[s], preferred_element_type=jnp.float32)
        mixed_ref[:, s, :] = mixed + own_prob * value_new
    each = heads // blocks
    for j, out in enumerate(outs):
        first = (me ^ j) * each
        for h in range(each):
            out[:, h * head : (h + 1) * head] = mixed_ref[first + h].astype(jnp.bfloat16)


def attend(pieces, cache_keys, cache_values, cache_lengths, width):
    seqs, slots, head = cache_keys.shape
    blocks, heads = len(pieces), width // head
    keys = pltpu.with_memory_space_constraint(cache_keys, pltpu.VMEM)
    values = pltpu.with_memory_space_constraint(cache_values, pltpu.VMEM)
    return call(
        functools.partial(attend_body, blocks, heads),
        [struct((seqs, width // blocks))] * blocks,
        [SMEM] + [VMEM] * (blocks + 2),
        [cache_lengths, *pieces, keys, values],
        limit=12,
        scratch=[
            pltpu.VMEM((seqs, width + 2 * head), jnp.float32),
            pltpu.VMEM((heads, seqs, head), jnp.float32),
            pltpu.VMEM((heads, seqs, head), jnp.float32),
        ],
        flops=4 * seqs * heads * head * slots,
        traffic=4 * seqs * slots * head,
    )


def place_body(n, *refs):
    pieces, out_ref = refs[:n], refs[n]
    me = lax.axis_index("gx")
    total = pieces[0][...]
    for p in pieces[1:]:
        total = total + p[...].astype(jnp.float32)
    each = out_ref.shape[1]
    for k in range(out_ref.shape[0]):
        out_ref[me ^ k] = total[k * each : (k + 1) * each].astype(jnp.bfloat16)


def shards(tokens, gain, w_qkv, w_out, cache_keys, cache_values, cache_lengths):
    groups, blocks = lax.axis_size("gx"), lax.axis_size("yz")
    seqs, depth = tokens.shape[0], w_qkv.shape[0]
    width = w_out.shape[0] * blocks
    normed = call(
        norm_body,
        [struct((seqs, depth))] * groups,
        [VMEM, VMEM],
        [tokens, gain.reshape(1, -1)],
    )
    mine = jnp.concatenate(exchange(normed, "gx"), axis=0)
    w_near = load(w_qkv, mine)
    pieces = exchange([mine] * blocks, "yz")
    sums = exchange(project(pieces, w_near, 640), "gx")
    parts = call(
        total_body, [struct((seqs, w_qkv.shape[1]))] * blocks, [VMEM] * groups, sums
    )
    attended = attend(exchange(parts, "yz"), cache_keys, cache_values, cache_lengths, width)
    mine = jnp.concatenate(exchange(attended, "yz"), axis=0)
    w_near = load(w_out, mine)
    pieces = exchange([mine] * groups, "gx")
    sums = exchange(project(pieces, w_near, 512), "yz")
    return call(
        functools.partial(place_body, blocks),
        struct((groups, seqs, w_out.shape[1])),
        [VMEM] * blocks,
        sums,
    )


def attend_local(qkv, cache_keys, cache_values, cache_lengths, width):
    seq_rows = qkv.shape[0]
    head = cache_keys.shape[2]
    slots = cache_keys.shape[1]
    scale = 1.0 / jnp.sqrt(jnp.float32(head))
    query = qkv[:, :width].reshape(seq_rows, width // head, head)
    key_new = qkv[:, width : width + head]
    value_new = qkv[:, width + head :]
    scores = (
        jnp.einsum("shd,std->sht", query, cache_keys, preferred_element_type=jnp.float32) * scale
    )
    own = jnp.einsum("shd,sd->sh", query, key_new, preferred_element_type=jnp.float32) * scale
    valid = jnp.arange(slots, dtype=jnp.int32)[None, None, :] < cache_lengths[:, None, None]
    masked = jnp.where(valid, scores, -jnp.inf)
    top = jnp.maximum(jnp.max(masked, axis=2), own)
    weights = jnp.where(valid, jnp.exp(masked - top[:, :, None]), 0.0)
    own_weight = jnp.exp(own - top)
    total = jnp.sum(weights, axis=2) + own_weight
    probs = (weights / total[:, :, None]).astype(jnp.bfloat16)
    own_prob = (own_weight / total).astype(jnp.bfloat16)
    mixed = jnp.einsum("sht,std->shd", probs, cache_values, preferred_element_type=jnp.float32)
    mixed = (
        mixed + own_prob.astype(jnp.float32)[:, :, None] * value_new.astype(jnp.float32)[:, None, :]
    )
    return mixed.reshape(seq_rows, width).astype(jnp.bfloat16)


def shards_any(tokens, gain, w_qkv, w_out, cache_keys, cache_values, cache_lengths):
    seq_rows = tokens.shape[0]
    groups = lax.axis_size("gx")
    blocks = lax.axis_size("yz")
    width = w_out.shape[0] * blocks
    xf = tokens.astype(jnp.float32)
    mean = jnp.mean(xf, axis=1, keepdims=True)
    centered = xf - mean
    variance = jnp.mean(centered * centered, axis=1, keepdims=True)
    normed = (centered / jnp.sqrt(variance + 1e-05) * gain[None, :]).astype(jnp.bfloat16)
    feature_rows = lax.all_to_all(normed, "gx", split_axis=1, concat_axis=0, tiled=True)
    column_count = w_qkv.shape[1]
    partial_value = jnp.dot(
        lax.all_gather(feature_rows, "yz", axis=0, tiled=True),
        w_qkv,
        preferred_element_type=jnp.float32,
    )
    partial_value = partial_value.reshape(blocks, groups, seq_rows, column_count)
    summed = lax.psum_scatter(partial_value, "gx", scatter_dimension=1, tiled=True)
    summed = summed.reshape(blocks, seq_rows, column_count).astype(jnp.bfloat16)
    received = lax.all_to_all(summed, "yz", split_axis=0, concat_axis=0, tiled=True)
    qkv = received.transpose(1, 0, 2).reshape(seq_rows, blocks * column_count)
    attended = attend_local(qkv, cache_keys, cache_values, cache_lengths, width)
    feature_block = w_out.shape[0]
    split = attended.reshape(seq_rows, blocks, feature_block)
    received = lax.all_to_all(split, "yz", split_axis=1, concat_axis=0, tiled=True)
    received = received.reshape(blocks * seq_rows, feature_block)
    everyone = lax.all_gather(received, "gx", axis=0, tiled=True)
    everyone = everyone.reshape(groups, blocks * seq_rows, feature_block)
    summed = lax.psum_scatter(
        jnp.einsum("gcf,fd->cgd", everyone, w_out, preferred_element_type=jnp.float32),
        "yz",
        scatter_dimension=0,
        tiled=True,
    )
    return summed.transpose(1, 0, 2).astype(jnp.bfloat16)


def solution(mesh):
    placed = (
        P(("parts", "gx", "yz"), None),
        P(),
        P("gx", "yz"),
        P("yz", "gx"),
        P(("parts", "gx", "yz"), None, None),
        P(("parts", "gx", "yz"), None, None),
        P(("parts", "gx", "yz")),
    )
    small = mesh.shape["gx"] == 4 and mesh.shape["yz"] == 4
    return jax.shard_map(
        shards if small else shards_any,
        mesh=mesh,
        in_specs=placed,
        out_specs=P(None, ("parts", "yz"), "gx"),
        check_vma=False,
    )
```

```python
import functools

import jax
import jax.numpy as jnp
from jax import lax
from jax.experimental import pallas as pl
from jax.experimental.pallas import tpu as pltpu
from jax.sharding import PartitionSpec as P

VMEM = pl.BlockSpec(memory_space=pltpu.VMEM)
SMEM = pl.BlockSpec(memory_space=pltpu.SMEM)
ANY = pl.BlockSpec(memory_space=pl.ANY)
MIB = 1 << 20
NEAR_LAST = (0, 3, 2, 1)
FAR_LAST = (0, 2, 1, 3)


def call(body, outs, in_specs, args, limit=8, scratch=(), flops=0, traffic=0, order=()):
    order = [*order, *range(len(order), len(args))]

    def ordered(*refs):
        ins = [refs[order.index(i)] for i in range(len(args))]
        body(*ins, *refs[len(args) :])

    return pl.pallas_call(
        ordered,
        out_shape=outs,
        in_specs=[in_specs[i] for i in order],
        out_specs=jax.tree.map(lambda _: VMEM, outs),
        scratch_shapes=scratch,
        compiler_params=pltpu.CompilerParams(vmem_limit_bytes=limit * MIB),
        cost_estimate=pl.CostEstimate(flops=flops, bytes_accessed=traffic, transcendentals=0),
    )(*[args[i] for i in order])


def far(x):
    return pltpu.with_memory_space_constraint(x, pltpu.HBM)


def struct(shape, dtype=jnp.bfloat16):
    return jax.ShapeDtypeStruct(shape, dtype)


def exchange(pieces, axis):
    size = lax.axis_size(axis)
    return [pieces[0]] + [
        lax.ppermute(pieces[k], axis, [(i, i ^ k) for i in range(size)]) for k in range(1, size)
    ]


def norm_body(x_hbm, gain_hbm, *refs):
    *out_refs, x_ref, gain_ref, sems = refs
    copies = [
        pltpu.make_async_copy(x_hbm, x_ref, sems.at[0]),
        pltpu.make_async_copy(gain_hbm, gain_ref, sems.at[1]),
    ]
    for copy in copies:
        copy.start()
    block = out_refs[0].shape[1]
    me = lax.axis_index("gx")
    copies[0].wait()
    x = x_ref[...].astype(jnp.float32)
    mean = jnp.mean(x, axis=1, keepdims=True)
    centered = x - mean
    variance = jnp.mean(centered * centered, axis=1, keepdims=True)
    inverse = 1.0 / jnp.sqrt(variance + 1e-05)
    copies[1].wait()
    for k, out_ref in enumerate(out_refs):
        columns = pl.ds(pl.multiple_of((me ^ k) * block, 128), block)
        part = x_ref[:, columns].astype(jnp.float32) - mean
        out_ref[...] = (part * inverse * gain_ref[:, columns]).astype(jnp.bfloat16)


def project_body(tile, n, *refs):
    pieces, w_ref, outs = refs[:n], refs[n], refs[n + 1 :]
    rows = jnp.concatenate([p[...] for p in pieces], axis=0)
    width = w_ref.shape[1]
    each = rows.shape[0] // (n * n)

    @pl.loop(0, width // tile)
    def _(i):
        columns = pl.ds(pl.multiple_of(i * tile, 128), tile)
        total = jnp.dot(rows, w_ref[:, columns], preferred_element_type=jnp.float32)
        for k, out in enumerate(outs):
            group = [
                total[(j * n + k) * each : (j * n + k + 1) * each] for j in range(n)
            ]
            out[:, columns] = jnp.concatenate(group, axis=0).astype(out.dtype)


def project(pieces, w, tile, order):
    n = len(pieces)
    rows, width = pieces[0].shape[0], w.shape[1]
    outs = [struct((rows, width), jnp.float32 if k == 0 else jnp.bfloat16) for k in range(n)]
    w = pltpu.with_memory_space_constraint(w, pltpu.VMEM)
    return call(
        functools.partial(project_body, tile, n),
        outs,
        [VMEM] * (n + 1),
        [*pieces, w],
        limit=12,
        flops=2 * n * rows * w.shape[0] * width,
        traffic=2 * w.shape[0] * width,
        order=order,
    )


def total_body(*refs):
    ins, outs = refs[: len(refs) // 2], refs[len(refs) // 2 :]
    total = ins[0][...]
    for r in ins[1:]:
        total = total + r[...].astype(jnp.float32)
    each = outs[0].shape[0]
    for j, out in enumerate(outs):
        out[...] = total[j * each : (j + 1) * each].astype(jnp.bfloat16)


def attend_body(blocks, heads, *refs):
    pieces, (key_ref, value_ref, length_ref) = refs[:blocks], refs[blocks : blocks + 3]
    outs = refs[blocks + 3 : 2 * blocks + 3]
    row_ref, query_ref, mixed_ref = refs[2 * blocks + 3 :]
    me = lax.axis_index("yz")
    part = pieces[0].shape[1]
    seqs, slots, head = key_ref.shape
    scale = 1.0 / jnp.sqrt(jnp.float32(head))
    for j, piece in enumerate(pieces):
        row_ref[:, pl.ds(pl.multiple_of((me ^ j) * part, 128), part)] = piece[...].astype(jnp.float32)
    for h in range(heads):
        query_ref[h] = row_ref[:, h * head : (h + 1) * head]
    slot = lax.broadcasted_iota(jnp.int32, (1, slots), 1)
    width = heads * head
    queries = [query_ref[:, s, :] for s in range(seqs)]
    owns = [
        jnp.sum(queries[s] * row_ref[s : s + 1, width : width + head], axis=1, keepdims=True) * scale
        for s in range(seqs)
    ]
    scores = [
        lax.dot_general(
            queries[s].astype(jnp.bfloat16),
            key_ref[s],
            (((1,), (1,)), ((), ())),
            preferred_element_type=jnp.float32,
        )
        for s in range(seqs)
    ]
    masked = [jnp.where(slot < length_ref[s], scores[s] * scale, -jnp.inf) for s in range(seqs)]
    tops = [jnp.maximum(jnp.max(masked[s], axis=1, keepdims=True), owns[s]) for s in range(seqs)]
    weights = [jnp.exp(masked[s] - tops[s]) for s in range(seqs)]
    own_weights = [jnp.exp(owns[s] - tops[s]) for s in range(seqs)]
    totals = [jnp.sum(weights[s], axis=1, keepdims=True) + own_weights[s] for s in range(seqs)]
    probs = [(weights[s] / totals[s]).astype(jnp.bfloat16) for s in range(seqs)]
    mixed = [
        jnp.dot(probs[s], value_ref[s], preferred_element_type=jnp.float32) for s in range(seqs)
    ]
    for s in range(seqs):
        own_prob = (own_weights[s] / totals[s]).astype(jnp.bfloat16).astype(jnp.float32)
        value_new = row_ref[s : s + 1, width + head : width + 2 * head]
        mixed_ref[:, s, :] = mixed[s] + own_prob * value_new
    each = heads // blocks
    for j, out in enumerate(outs):
        first = (me ^ j) * each
        for h in range(each):
            out[:, h * head : (h + 1) * head] = mixed_ref[first + h].astype(jnp.bfloat16)


def attend(pieces, cache_keys, cache_values, cache_lengths, width):
    seqs, slots, head = cache_keys.shape
    blocks, heads = len(pieces), width // head
    keys = pltpu.with_memory_space_constraint(cache_keys, pltpu.VMEM)
    values = pltpu.with_memory_space_constraint(cache_values, pltpu.VMEM)
    return call(
        functools.partial(attend_body, blocks, heads),
        [struct((seqs, width // blocks))] * blocks,
        [VMEM] * (blocks + 2) + [SMEM],
        [*pieces, keys, values, cache_lengths],
        order=NEAR_LAST,
        limit=12,
        scratch=[
            pltpu.VMEM((seqs, width + 2 * head), jnp.float32),
            pltpu.VMEM((heads, seqs, head), jnp.float32),
            pltpu.VMEM((heads, seqs, head), jnp.float32),
        ],
        flops=50_000_000_000,
        traffic=4 * seqs * slots * head,
    )


def join_body(*refs):
    refs[-1][...] = jnp.concatenate([r[...] for r in refs[:-1]], axis=0)


def place_body(n, *refs):
    pieces, out_ref = refs[:n], refs[n]
    me = lax.axis_index("gx")
    total = pieces[0][...]
    for p in pieces[1:]:
        total = total + p[...].astype(jnp.float32)
    each = out_ref.shape[1]
    for k in range(out_ref.shape[0]):
        out_ref[me ^ k] = total[k * each : (k + 1) * each].astype(jnp.bfloat16)


def shards(tokens, gain, w_qkv, w_out, cache_keys, cache_values, cache_lengths):
    groups, blocks = lax.axis_size("gx"), lax.axis_size("yz")
    seqs, depth = tokens.shape[0], w_qkv.shape[0]
    width = w_out.shape[0] * blocks
    normed = call(
        norm_body,
        [struct((seqs, depth))] * groups,
        [ANY, ANY],
        [far(tokens), far(gain.reshape(1, -1))],
        scratch=[
            pltpu.VMEM(tokens.shape, tokens.dtype),
            pltpu.VMEM((1, gain.shape[0]), gain.dtype),
            pltpu.SemaphoreType.DMA((2,)),
        ],
        flops=50_000_000_000,
    )
    mine = call(join_body, struct((groups * seqs, depth)), [VMEM] * groups, exchange(normed, "gx"), order=NEAR_LAST)
    pieces = exchange([mine] * blocks, "yz")
    sums = exchange(project(pieces, w_qkv, w_qkv.shape[1], FAR_LAST), "gx")
    parts = call(
        total_body, [struct((seqs, w_qkv.shape[1]))] * blocks, [VMEM] * groups, sums, order=NEAR_LAST
    )
    attended = attend(exchange(parts, "yz"), cache_keys, cache_values, cache_lengths, width)
    got = exchange(attended, "yz")
    mine = call(join_body, struct((4 * seqs, got[0].shape[1])), [VMEM] * 4, got, flops=50_000_000_000, order=NEAR_LAST)
    pieces = exchange([mine] * groups, "gx")
    sums = exchange(project(pieces, w_out, w_out.shape[1], NEAR_LAST), "yz")
    return call(
        functools.partial(place_body, blocks),
        struct((groups, seqs, w_out.shape[1])),
        [VMEM] * blocks,
        sums,
        order=FAR_LAST,
    )


def attend_local(qkv, cache_keys, cache_values, cache_lengths, width):
    seq_rows = qkv.shape[0]
    head = cache_keys.shape[2]
    slots = cache_keys.shape[1]
    scale = 1.0 / jnp.sqrt(jnp.float32(head))
    query = qkv[:, :width].reshape(seq_rows, width // head, head)
    key_new = qkv[:, width : width + head]
    value_new = qkv[:, width + head :]
    scores = (
        jnp.einsum("shd,std->sht", query, cache_keys, preferred_element_type=jnp.float32) * scale
    )
    own = jnp.einsum("shd,sd->sh", query, key_new, preferred_element_type=jnp.float32) * scale
    valid = jnp.arange(slots, dtype=jnp.int32)[None, None, :] < cache_lengths[:, None, None]
    masked = jnp.where(valid, scores, -jnp.inf)
    top = jnp.maximum(jnp.max(masked, axis=2), own)
    weights = jnp.where(valid, jnp.exp(masked - top[:, :, None]), 0.0)
    own_weight = jnp.exp(own - top)
    total = jnp.sum(weights, axis=2) + own_weight
    probs = (weights / total[:, :, None]).astype(jnp.bfloat16)
    own_prob = (own_weight / total).astype(jnp.bfloat16)
    mixed = jnp.einsum("sht,std->shd", probs, cache_values, preferred_element_type=jnp.float32)
    mixed = (
        mixed + own_prob.astype(jnp.float32)[:, :, None] * value_new.astype(jnp.float32)[:, None, :]
    )
    return mixed.reshape(seq_rows, width).astype(jnp.bfloat16)


def shards_any(tokens, gain, w_qkv, w_out, cache_keys, cache_values, cache_lengths):
    seq_rows = tokens.shape[0]
    groups = lax.axis_size("gx")
    blocks = lax.axis_size("yz")
    width = w_out.shape[0] * blocks
    xf = tokens.astype(jnp.float32)
    mean = jnp.mean(xf, axis=1, keepdims=True)
    centered = xf - mean
    variance = jnp.mean(centered * centered, axis=1, keepdims=True)
    normed = (centered / jnp.sqrt(variance + 1e-05) * gain[None, :]).astype(jnp.bfloat16)
    feature_rows = lax.all_to_all(normed, "gx", split_axis=1, concat_axis=0, tiled=True)
    column_count = w_qkv.shape[1]
    partial_value = jnp.dot(
        lax.all_gather(feature_rows, "yz", axis=0, tiled=True),
        w_qkv,
        preferred_element_type=jnp.float32,
    )
    partial_value = partial_value.reshape(blocks, groups, seq_rows, column_count)
    summed = lax.psum_scatter(partial_value, "gx", scatter_dimension=1, tiled=True)
    summed = summed.reshape(blocks, seq_rows, column_count).astype(jnp.bfloat16)
    received = lax.all_to_all(summed, "yz", split_axis=0, concat_axis=0, tiled=True)
    qkv = received.transpose(1, 0, 2).reshape(seq_rows, blocks * column_count)
    attended = attend_local(qkv, cache_keys, cache_values, cache_lengths, width)
    feature_block = w_out.shape[0]
    split = attended.reshape(seq_rows, blocks, feature_block)
    received = lax.all_to_all(split, "yz", split_axis=1, concat_axis=0, tiled=True)
    received = received.reshape(blocks * seq_rows, feature_block)
    everyone = lax.all_gather(received, "gx", axis=0, tiled=True)
    everyone = everyone.reshape(groups, blocks * seq_rows, feature_block)
    summed = lax.psum_scatter(
        jnp.einsum("gcf,fd->cgd", everyone, w_out, preferred_element_type=jnp.float32),
        "yz",
        scatter_dimension=0,
        tiled=True,
    )
    return summed.transpose(1, 0, 2).astype(jnp.bfloat16)


def solution(mesh):
    placed = (
        P(("parts", "gx", "yz"), None),
        P(),
        P("gx", "yz"),
        P("yz", "gx"),
        P(("parts", "gx", "yz"), None, None),
        P(("parts", "gx", "yz"), None, None),
        P(("parts", "gx", "yz")),
    )
    small = mesh.shape["gx"] == 4 and mesh.shape["yz"] == 4
    return jax.shard_map(
        shards if small else shards_any,
        mesh=mesh,
        in_specs=placed,
        out_specs=P(None, ("parts", "yz"), "gx"),
        check_vma=False,
    )
```

```python
import functools

import jax
import jax.numpy as jnp
from jax import lax
from jax.experimental import pallas as pl
from jax.experimental.pallas import tpu as pltpu
from jax.sharding import PartitionSpec as P

VMEM = pl.BlockSpec(memory_space=pltpu.VMEM)
SMEM = pl.BlockSpec(memory_space=pltpu.SMEM)
ANY = pl.BlockSpec(memory_space=pl.ANY)
MIB = 1 << 20
A1 = (0, 1, 3, 2)
A2 = (0, 1, 2, 3, 4, 5)
B1 = (0, 2, 1, 3)
B2 = (0, 2, 3, 1)
C1 = (0, 3, 2, 1)
C2 = (0, 1, 2, 3)
D = (0, 2, 1, 3)


def call(body, outs, in_specs, args, limit=8, scratch=(), flops=0, traffic=0, order=()):
    order = [*order, *range(len(order), len(args))]

    def ordered(*refs):
        ins = [refs[order.index(i)] for i in range(len(args))]
        body(*ins, *refs[len(args) :])

    return pl.pallas_call(
        ordered,
        out_shape=outs,
        in_specs=[in_specs[i] for i in order],
        out_specs=jax.tree.map(lambda _: VMEM, outs),
        scratch_shapes=scratch,
        compiler_params=pltpu.CompilerParams(vmem_limit_bytes=limit * MIB),
        cost_estimate=pl.CostEstimate(flops=flops, bytes_accessed=traffic, transcendentals=0),
    )(*[args[i] for i in order])


def near(x):
    return pltpu.with_memory_space_constraint(x, pltpu.VMEM)


def far(x):
    return pltpu.with_memory_space_constraint(x, pltpu.HBM)


def struct(shape, dtype=jnp.bfloat16):
    return jax.ShapeDtypeStruct(shape, dtype)


def exchange(pieces, axis):
    size = lax.axis_size(axis)
    return [pieces[0]] + [
        lax.ppermute(pieces[k], axis, [(i, i ^ k) for i in range(size)]) for k in range(1, size)
    ]


def swap(piece, axis, k):
    return lax.ppermute(piece, axis, [(i, i ^ k) for i in range(lax.axis_size(axis))])


def norm_body(x_hbm, gain_hbm, *refs):
    *out_refs, x_ref, gain_ref, sems = refs
    copies = [
        pltpu.make_async_copy(x_hbm, x_ref, sems.at[0]),
        pltpu.make_async_copy(gain_hbm, gain_ref, sems.at[1]),
    ]
    for copy in copies:
        copy.start()
    block = out_refs[0].shape[1]
    me = lax.axis_index("gx")
    copies[0].wait()
    x = x_ref[...].astype(jnp.float32)
    mean = jnp.mean(x, axis=1, keepdims=True)
    centered = x - mean
    variance = jnp.mean(centered * centered, axis=1, keepdims=True)
    inverse = 1.0 / jnp.sqrt(variance + 1e-05)
    copies[1].wait()
    for k, out_ref in enumerate(out_refs):
        columns = pl.ds(pl.multiple_of((me ^ k) * block, 128), block)
        part = x_ref[:, columns].astype(jnp.float32) - mean
        out_ref[...] = (part * inverse * gain_ref[:, columns]).astype(jnp.bfloat16)


def regroup(total, n):
    each = total.shape[0] // (n * n)
    return [
        jnp.concatenate(
            [total[(j * n + k) * each : (j * n + k + 1) * each] for j in range(n)], axis=0
        )
        for k in range(n)
    ]


def dot_body(cuts, parts, *refs):
    refs = list(refs)
    pieces = [jnp.concatenate([refs.pop(0)[...] for _ in range(n)], axis=1) for n in cuts]
    w_ref, *outs = refs
    total = jnp.dot(
        jnp.concatenate(pieces, axis=0), w_ref[...], preferred_element_type=jnp.float32
    )
    for group, n in zip(regroup(total, len(cuts)), parts):
        for i in range(n):
            out = outs.pop(0)
            width = out.shape[1]
            out[...] = group[:, i * width : (i + 1) * width].astype(out.dtype)


def dot(pieces, w, kept=(0,), parts=(1, 1, 1, 1), order=()):
    n, rows, (depth, width) = len(pieces), pieces[0][0].shape[0], w.shape
    outs = [
        struct((rows, width // parts[k]), jnp.float32 if k in kept else jnp.bfloat16)
        for k in range(n)
        for _ in range(parts[k])
    ]
    cuts = [len(piece) for piece in pieces]
    ins = [part for piece in pieces for part in piece]
    return call(
        functools.partial(dot_body, cuts, parts),
        outs,
        [VMEM] * (len(ins) + 1),
        [*ins, near(w)],
        limit=6,
        flops=2 * n * rows * depth * width,
        traffic=2 * depth * width,
        order=order,
    )


def total_body(*refs):
    ins, outs = refs[: len(refs) // 2], refs[len(refs) // 2 :]
    total = ins[0][...]
    for r in ins[1:]:
        total = total + r[...].astype(jnp.float32)
    each = outs[0].shape[0]
    for j, out in enumerate(outs):
        out[...] = total[j * each : (j + 1) * each].astype(jnp.bfloat16)


def attend_body(blocks, heads, *refs):
    pieces, (key_ref, value_ref, length_ref) = refs[:blocks], refs[blocks : blocks + 3]
    outs = refs[blocks + 3 : 2 * blocks + 3]
    row_ref, query_ref, mixed_ref = refs[2 * blocks + 3 :]
    me = lax.axis_index("yz")
    part = pieces[0].shape[1]
    seqs, slots, head = key_ref.shape
    scale = 1.0 / jnp.sqrt(jnp.float32(head))
    for j, piece in enumerate(pieces):
        row_ref[:, pl.ds(pl.multiple_of((me ^ j) * part, 128), part)] = piece[...].astype(jnp.float32)
    for h in range(heads):
        query_ref[h] = row_ref[:, h * head : (h + 1) * head]
    slot = lax.broadcasted_iota(jnp.int32, (1, slots), 1)
    width = heads * head
    queries = [query_ref[:, s, :] for s in range(seqs)]
    owns = [
        jnp.sum(queries[s] * row_ref[s : s + 1, width : width + head], axis=1, keepdims=True) * scale
        for s in range(seqs)
    ]
    scores = [
        lax.dot_general(
            queries[s].astype(jnp.bfloat16),
            key_ref[s],
            (((1,), (1,)), ((), ())),
            preferred_element_type=jnp.float32,
        )
        for s in range(seqs)
    ]
    masked = [jnp.where(slot < length_ref[s], scores[s] * scale, -jnp.inf) for s in range(seqs)]
    tops = [jnp.maximum(jnp.max(masked[s], axis=1, keepdims=True), owns[s]) for s in range(seqs)]
    weights = [jnp.exp(masked[s] - tops[s]) for s in range(seqs)]
    own_weights = [jnp.exp(owns[s] - tops[s]) for s in range(seqs)]
    totals = [jnp.sum(weights[s], axis=1, keepdims=True) + own_weights[s] for s in range(seqs)]
    probs = [(weights[s] / totals[s]).astype(jnp.bfloat16) for s in range(seqs)]
    mixed = [
        jnp.dot(probs[s], value_ref[s], preferred_element_type=jnp.float32) for s in range(seqs)
    ]
    for s in range(seqs):
        own_prob = (own_weights[s] / totals[s]).astype(jnp.bfloat16).astype(jnp.float32)
        value_new = row_ref[s : s + 1, width + head : width + 2 * head]
        mixed_ref[:, s, :] = mixed[s] + own_prob * value_new
    each = heads // blocks
    for j, out in enumerate(outs):
        first = (me ^ j) * each
        for h in range(each):
            out[:, h * head : (h + 1) * head] = mixed_ref[first + h].astype(jnp.bfloat16)


def attend(pieces, cache_keys, cache_values, cache_lengths, width):
    seqs, slots, head = cache_keys.shape
    blocks, heads = len(pieces), width // head
    keys = pltpu.with_memory_space_constraint(cache_keys, pltpu.VMEM)
    values = pltpu.with_memory_space_constraint(cache_values, pltpu.VMEM)
    return call(
        functools.partial(attend_body, blocks, heads),
        [struct((seqs, width // blocks))] * blocks,
        [VMEM] * (blocks + 2) + [SMEM],
        [*pieces, keys, values, cache_lengths],
        order=B2,
        limit=12,
        scratch=[
            pltpu.VMEM((seqs, width + 2 * head), jnp.float32),
            pltpu.VMEM((heads, seqs, head), jnp.float32),
            pltpu.VMEM((heads, seqs, head), jnp.float32),
        ],
        flops=50_000_000_000,
        traffic=4 * seqs * slots * head,
    )


def cut_body(*refs):
    rows = jnp.concatenate([r[...] for r in refs[:4]], axis=0)
    whole, early, late = refs[4:]
    whole[...] = rows
    early[...] = rows[:, : early.shape[1]]
    late[...] = rows[:, early.shape[1] :]


def join_body(*refs):
    refs[-1][...] = jnp.concatenate([r[...] for r in refs[:-1]], axis=0)


def place_body(n, *refs):
    pieces, out_ref = refs[:n], refs[n]
    me = lax.axis_index("gx")
    total = pieces[0][...]
    for p in pieces[1:]:
        total = total + p[...].astype(jnp.float32)
    each = out_ref.shape[1]
    for k in range(out_ref.shape[0]):
        out_ref[me ^ k] = total[k * each : (k + 1) * each].astype(jnp.bfloat16)


def shards(tokens, gain, w_qkv, w_out, cache_keys, cache_values, cache_lengths):
    groups, blocks = lax.axis_size("gx"), lax.axis_size("yz")
    seqs, depth = tokens.shape[0], w_qkv.shape[0]
    width = w_out.shape[0] * blocks
    normed = call(
        norm_body,
        [struct((seqs, depth))] * groups,
        [ANY, ANY],
        [far(tokens), far(gain.reshape(1, -1))],
        scratch=[
            pltpu.VMEM(tokens.shape, tokens.dtype),
            pltpu.VMEM((1, gain.shape[0]), gain.dtype),
            pltpu.SemaphoreType.DMA((2,)),
        ],
        flops=50_000_000_000,
    )
    half = depth // 2
    mine, *halves = call(
        cut_body,
        [struct((groups * seqs, size)) for size in (depth, half, half)],
        [VMEM] * groups,
        exchange(normed, "gx"),
        order=A1,
    )
    one = swap(mine, "yz", 1)
    two = [swap(part, "yz", 2) for part in halves]
    three = [swap(part, "yz", 1) for part in two]
    sums = dot([[mine], [one], two, three], w_qkv, order=A2)
    sums = exchange(sums, "gx")
    parts = call(
        total_body, [struct((seqs, w_qkv.shape[1]))] * blocks, [VMEM] * groups, sums, order=B1
    )
    attended = attend(exchange(parts, "yz"), cache_keys, cache_values, cache_lengths, width)
    got = exchange(attended, "yz")
    mine = call(join_body, struct((4 * seqs, got[0].shape[1])), [VMEM] * 4, got, flops=50_000_000_000, order=C1)
    two = swap(mine, "gx", 2)
    pieces = [[mine], [swap(mine, "gx", 1)], [two], [swap(two, "gx", 1)]]
    sums = exchange(dot(pieces, w_out, order=C2), "yz")
    return call(
        functools.partial(place_body, blocks),
        struct((groups, seqs, w_out.shape[1])),
        [VMEM] * blocks,
        sums,
        order=D,
    )


def attend_local(qkv, cache_keys, cache_values, cache_lengths, width):
    seq_rows = qkv.shape[0]
    head = cache_keys.shape[2]
    slots = cache_keys.shape[1]
    scale = 1.0 / jnp.sqrt(jnp.float32(head))
    query = qkv[:, :width].reshape(seq_rows, width // head, head)
    key_new = qkv[:, width : width + head]
    value_new = qkv[:, width + head :]
    scores = (
        jnp.einsum("shd,std->sht", query, cache_keys, preferred_element_type=jnp.float32) * scale
    )
    own = jnp.einsum("shd,sd->sh", query, key_new, preferred_element_type=jnp.float32) * scale
    valid = jnp.arange(slots, dtype=jnp.int32)[None, None, :] < cache_lengths[:, None, None]
    masked = jnp.where(valid, scores, -jnp.inf)
    top = jnp.maximum(jnp.max(masked, axis=2), own)
    weights = jnp.where(valid, jnp.exp(masked - top[:, :, None]), 0.0)
    own_weight = jnp.exp(own - top)
    total = jnp.sum(weights, axis=2) + own_weight
    probs = (weights / total[:, :, None]).astype(jnp.bfloat16)
    own_prob = (own_weight / total).astype(jnp.bfloat16)
    mixed = jnp.einsum("sht,std->shd", probs, cache_values, preferred_element_type=jnp.float32)
    mixed = (
        mixed + own_prob.astype(jnp.float32)[:, :, None] * value_new.astype(jnp.float32)[:, None, :]
    )
    return mixed.reshape(seq_rows, width).astype(jnp.bfloat16)


def shards_any(tokens, gain, w_qkv, w_out, cache_keys, cache_values, cache_lengths):
    seq_rows = tokens.shape[0]
    groups = lax.axis_size("gx")
    blocks = lax.axis_size("yz")
    width = w_out.shape[0] * blocks
    xf = tokens.astype(jnp.float32)
    mean = jnp.mean(xf, axis=1, keepdims=True)
    centered = xf - mean
    variance = jnp.mean(centered * centered, axis=1, keepdims=True)
    normed = (centered / jnp.sqrt(variance + 1e-05) * gain[None, :]).astype(jnp.bfloat16)
    feature_rows = lax.all_to_all(normed, "gx", split_axis=1, concat_axis=0, tiled=True)
    column_count = w_qkv.shape[1]
    partial_value = jnp.dot(
        lax.all_gather(feature_rows, "yz", axis=0, tiled=True),
        w_qkv,
        preferred_element_type=jnp.float32,
    )
    partial_value = partial_value.reshape(blocks, groups, seq_rows, column_count)
    summed = lax.psum_scatter(partial_value, "gx", scatter_dimension=1, tiled=True)
    summed = summed.reshape(blocks, seq_rows, column_count).astype(jnp.bfloat16)
    received = lax.all_to_all(summed, "yz", split_axis=0, concat_axis=0, tiled=True)
    qkv = received.transpose(1, 0, 2).reshape(seq_rows, blocks * column_count)
    attended = attend_local(qkv, cache_keys, cache_values, cache_lengths, width)
    feature_block = w_out.shape[0]
    split = attended.reshape(seq_rows, blocks, feature_block)
    received = lax.all_to_all(split, "yz", split_axis=1, concat_axis=0, tiled=True)
    received = received.reshape(blocks * seq_rows, feature_block)
    everyone = lax.all_gather(received, "gx", axis=0, tiled=True)
    everyone = everyone.reshape(groups, blocks * seq_rows, feature_block)
    summed = lax.psum_scatter(
        jnp.einsum("gcf,fd->cgd", everyone, w_out, preferred_element_type=jnp.float32),
        "yz",
        scatter_dimension=0,
        tiled=True,
    )
    return summed.transpose(1, 0, 2).astype(jnp.bfloat16)


def solution(mesh):
    placed = (
        P(("parts", "gx", "yz"), None),
        P(),
        P("gx", "yz"),
        P("yz", "gx"),
        P(("parts", "gx", "yz"), None, None),
        P(("parts", "gx", "yz"), None, None),
        P(("parts", "gx", "yz")),
    )
    small = mesh.shape["gx"] == 4 and mesh.shape["yz"] == 4
    return jax.shard_map(
        shards if small else shards_any,
        mesh=mesh,
        in_specs=placed,
        out_specs=P(None, ("parts", "yz"), "gx"),
        check_vma=False,
    )
```

```python
import functools

import jax
import jax.numpy as jnp
from jax import lax
from jax.experimental import pallas as pl
from jax.experimental.pallas import tpu as pltpu
from jax.sharding import PartitionSpec as P

VMEM = pl.BlockSpec(memory_space=pltpu.VMEM)
SMEM = pl.BlockSpec(memory_space=pltpu.SMEM)
ANY = pl.BlockSpec(memory_space=pl.ANY)
MIB = 1 << 20
A1 = (0, 1, 3, 2)
A2 = (0, 1, 2, 3, 4, 5)
B1 = (0, 2, 1, 3)
B2 = (0, 2, 3, 1)
C1 = (0, 3, 2, 1)
C2 = (0, 1, 2, 3)
D = (0, 2, 1, 3)


def call(body, outs, in_specs, args, limit=8, scratch=(), flops=0, traffic=0, order=()):
    order = [*order, *range(len(order), len(args))]

    def ordered(*refs):
        ins = [refs[order.index(i)] for i in range(len(args))]
        body(*ins, *refs[len(args) :])

    return pl.pallas_call(
        ordered,
        out_shape=outs,
        in_specs=[in_specs[i] for i in order],
        out_specs=jax.tree.map(lambda _: VMEM, outs),
        scratch_shapes=scratch,
        compiler_params=pltpu.CompilerParams(vmem_limit_bytes=limit * MIB),
        cost_estimate=pl.CostEstimate(flops=flops, bytes_accessed=traffic, transcendentals=0),
    )(*[args[i] for i in order])


def near(x):
    return pltpu.with_memory_space_constraint(x, pltpu.VMEM)


def far(x):
    return pltpu.with_memory_space_constraint(x, pltpu.HBM)


def struct(shape, dtype=jnp.bfloat16):
    return jax.ShapeDtypeStruct(shape, dtype)


def exchange(pieces, axis):
    size = lax.axis_size(axis)
    return [pieces[0]] + [
        lax.ppermute(pieces[k], axis, [(i, i ^ k) for i in range(size)]) for k in range(1, size)
    ]


def swap(piece, axis, k):
    return lax.ppermute(piece, axis, [(i, i ^ k) for i in range(lax.axis_size(axis))])


def norm_body(x_hbm, gain_hbm, *refs):
    *out_refs, x_ref, gain_ref, sems = refs
    copies = [
        pltpu.make_async_copy(x_hbm, x_ref, sems.at[0]),
        pltpu.make_async_copy(gain_hbm, gain_ref, sems.at[1]),
    ]
    for copy in copies:
        copy.start()
    block = out_refs[0].shape[1]
    me = lax.axis_index("gx")
    copies[0].wait()
    x = x_ref[...].astype(jnp.float32)
    mean = jnp.mean(x, axis=1, keepdims=True)
    centered = x - mean
    variance = jnp.mean(centered * centered, axis=1, keepdims=True)
    inverse = 1.0 / jnp.sqrt(variance + 1e-05)
    copies[1].wait()
    for k, out_ref in enumerate(out_refs):
        columns = pl.ds(pl.multiple_of((me ^ k) * block, 128), block)
        part = x_ref[:, columns].astype(jnp.float32) - mean
        out_ref[...] = (part * inverse * gain_ref[:, columns]).astype(jnp.bfloat16)


def regroup(total, n):
    each = total.shape[0] // (n * n)
    return [
        jnp.concatenate(
            [total[(j * n + k) * each : (j * n + k + 1) * each] for j in range(n)], axis=0
        )
        for k in range(n)
    ]


def dot_body(cuts, *refs):
    refs = list(refs)
    pieces = [jnp.concatenate([refs.pop(0)[...] for _ in range(n)], axis=1) for n in cuts]
    w_ref, *outs = refs
    rows = jnp.concatenate(pieces, axis=0)
    size = rows.shape[1] // max(cuts)
    total = sum(
        jnp.dot(rows[:, at : at + size], w_ref[at : at + size], preferred_element_type=jnp.float32)
        for at in range(0, rows.shape[1], size)
    )
    for group, out in zip(regroup(total, len(cuts)), outs):
        out[...] = group.astype(out.dtype)


def dot(pieces, w, order=()):
    n, rows, (depth, width) = len(pieces), pieces[0][0].shape[0], w.shape
    outs = [struct((rows, width), jnp.bfloat16 if k else jnp.float32) for k in range(n)]
    ins = [part for piece in pieces for part in piece]
    return call(
        functools.partial(dot_body, [len(piece) for piece in pieces]),
        outs,
        [VMEM] * (len(ins) + 1),
        [*ins, near(w)],
        limit=6,
        flops=2 * n * rows * depth * width,
        traffic=2 * depth * width,
        order=order,
    )


def total_body(*refs):
    ins, outs = refs[: len(refs) // 2], refs[len(refs) // 2 :]
    total = ins[0][...]
    for r in ins[1:]:
        total = total + r[...].astype(jnp.float32)
    each = outs[0].shape[0]
    for j, out in enumerate(outs):
        out[...] = total[j * each : (j + 1) * each].astype(jnp.bfloat16)


def attend_body(blocks, heads, *refs):
    pieces, (key_ref, value_ref, length_ref) = refs[:blocks], refs[blocks : blocks + 3]
    outs = refs[blocks + 3 : 2 * blocks + 3]
    row_ref, query_ref, mixed_ref = refs[2 * blocks + 3 :]
    me = lax.axis_index("yz")
    part = pieces[0].shape[1]
    seqs, slots, head = key_ref.shape
    scale = 1.0 / jnp.sqrt(jnp.float32(head))
    for j, piece in enumerate(pieces):
        row_ref[:, pl.ds(pl.multiple_of((me ^ j) * part, 128), part)] = piece[...].astype(jnp.float32)
    for h in range(heads):
        query_ref[h] = row_ref[:, h * head : (h + 1) * head]
    slot = lax.broadcasted_iota(jnp.int32, (1, slots), 1)
    width = heads * head
    queries = [query_ref[:, s, :] for s in range(seqs)]
    owns = [
        jnp.sum(queries[s] * row_ref[s : s + 1, width : width + head], axis=1, keepdims=True) * scale
        for s in range(seqs)
    ]
    scores = [
        lax.dot_general(
            queries[s].astype(jnp.bfloat16),
            key_ref[s],
            (((1,), (1,)), ((), ())),
            preferred_element_type=jnp.float32,
        )
        for s in range(seqs)
    ]
    masked = [jnp.where(slot < length_ref[s], scores[s] * scale, -jnp.inf) for s in range(seqs)]
    tops = [jnp.maximum(jnp.max(masked[s], axis=1, keepdims=True), owns[s]) for s in range(seqs)]
    weights = [jnp.exp(masked[s] - tops[s]) for s in range(seqs)]
    own_weights = [jnp.exp(owns[s] - tops[s]) for s in range(seqs)]
    totals = [jnp.sum(weights[s], axis=1, keepdims=True) + own_weights[s] for s in range(seqs)]
    probs = [(weights[s] / totals[s]).astype(jnp.bfloat16) for s in range(seqs)]
    mixed = [
        jnp.dot(probs[s], value_ref[s], preferred_element_type=jnp.float32) for s in range(seqs)
    ]
    for s in range(seqs):
        own_prob = (own_weights[s] / totals[s]).astype(jnp.bfloat16).astype(jnp.float32)
        value_new = row_ref[s : s + 1, width + head : width + 2 * head]
        mixed_ref[:, s, :] = mixed[s] + own_prob * value_new
    each = heads // blocks
    for j, out in enumerate(outs):
        first = (me ^ j) * each
        for h in range(each):
            out[:, h * head : (h + 1) * head] = mixed_ref[first + h].astype(jnp.bfloat16)


def attend(pieces, cache_keys, cache_values, cache_lengths, width):
    seqs, slots, head = cache_keys.shape
    blocks, heads = len(pieces), width // head
    keys = pltpu.with_memory_space_constraint(cache_keys, pltpu.VMEM)
    values = pltpu.with_memory_space_constraint(cache_values, pltpu.VMEM)
    return call(
        functools.partial(attend_body, blocks, heads),
        [struct((seqs, width // blocks))] * blocks,
        [VMEM] * (blocks + 2) + [SMEM],
        [*pieces, keys, values, cache_lengths],
        order=B2,
        limit=12,
        scratch=[
            pltpu.VMEM((seqs, width + 2 * head), jnp.float32),
            pltpu.VMEM((heads, seqs, head), jnp.float32),
            pltpu.VMEM((heads, seqs, head), jnp.float32),
        ],
        flops=50_000_000_000,
        traffic=4 * seqs * slots * head,
    )


def cut_body(*refs):
    rows = jnp.concatenate([r[...] for r in refs[:4]], axis=0)
    whole, early, late = refs[4:]
    whole[...] = rows
    early[...] = rows[:, : early.shape[1]]
    late[...] = rows[:, early.shape[1] :]


def join_body(*refs):
    refs[-1][...] = jnp.concatenate([r[...] for r in refs[:-1]], axis=0)


def place_body(n, *refs):
    pieces, out_ref = refs[:n], refs[n]
    me = lax.axis_index("gx")
    total = pieces[0][...]
    for p in pieces[1:]:
        total = total + p[...].astype(jnp.float32)
    each = out_ref.shape[1]
    for k in range(out_ref.shape[0]):
        out_ref[me ^ k] = total[k * each : (k + 1) * each].astype(jnp.bfloat16)


def shards(tokens, gain, w_qkv, w_out, cache_keys, cache_values, cache_lengths):
    groups, blocks = lax.axis_size("gx"), lax.axis_size("yz")
    seqs, depth = tokens.shape[0], w_qkv.shape[0]
    width = w_out.shape[0] * blocks
    normed = call(
        norm_body,
        [struct((seqs, depth))] * groups,
        [ANY, ANY],
        [far(tokens), far(gain.reshape(1, -1))],
        scratch=[
            pltpu.VMEM(tokens.shape, tokens.dtype),
            pltpu.VMEM((1, gain.shape[0]), gain.dtype),
            pltpu.SemaphoreType.DMA((2,)),
        ],
        flops=50_000_000_000,
    )
    half = depth // 2
    mine, *halves = call(
        cut_body,
        [struct((groups * seqs, size)) for size in (depth, half, half)],
        [VMEM] * groups,
        exchange(normed, "gx"),
        order=A1,
    )
    one = swap(mine, "yz", 1)
    two = [swap(part, "yz", 2) for part in halves]
    three = [swap(part, "yz", 1) for part in two]
    sums = dot([[mine], [one], two, three], w_qkv, order=A2)
    sums = exchange(sums, "gx")
    parts = call(
        total_body, [struct((seqs, w_qkv.shape[1]))] * blocks, [VMEM] * groups, sums, order=B1
    )
    attended = attend(exchange(parts, "yz"), cache_keys, cache_values, cache_lengths, width)
    got = exchange(attended, "yz")
    mine = call(join_body, struct((4 * seqs, got[0].shape[1])), [VMEM] * 4, got, flops=50_000_000_000, order=C1)
    two = swap(mine, "gx", 2)
    pieces = [[mine], [swap(mine, "gx", 1)], [two], [swap(two, "gx", 1)]]
    sums = exchange(dot(pieces, w_out, order=C2), "yz")
    return call(
        functools.partial(place_body, blocks),
        struct((groups, seqs, w_out.shape[1])),
        [VMEM] * blocks,
        sums,
        order=D,
    )


def attend_local(qkv, cache_keys, cache_values, cache_lengths, width):
    seq_rows = qkv.shape[0]
    head = cache_keys.shape[2]
    slots = cache_keys.shape[1]
    scale = 1.0 / jnp.sqrt(jnp.float32(head))
    query = qkv[:, :width].reshape(seq_rows, width // head, head)
    key_new = qkv[:, width : width + head]
    value_new = qkv[:, width + head :]
    scores = (
        jnp.einsum("shd,std->sht", query, cache_keys, preferred_element_type=jnp.float32) * scale
    )
    own = jnp.einsum("shd,sd->sh", query, key_new, preferred_element_type=jnp.float32) * scale
    valid = jnp.arange(slots, dtype=jnp.int32)[None, None, :] < cache_lengths[:, None, None]
    masked = jnp.where(valid, scores, -jnp.inf)
    top = jnp.maximum(jnp.max(masked, axis=2), own)
    weights = jnp.where(valid, jnp.exp(masked - top[:, :, None]), 0.0)
    own_weight = jnp.exp(own - top)
    total = jnp.sum(weights, axis=2) + own_weight
    probs = (weights / total[:, :, None]).astype(jnp.bfloat16)
    own_prob = (own_weight / total).astype(jnp.bfloat16)
    mixed = jnp.einsum("sht,std->shd", probs, cache_values, preferred_element_type=jnp.float32)
    mixed = (
        mixed + own_prob.astype(jnp.float32)[:, :, None] * value_new.astype(jnp.float32)[:, None, :]
    )
    return mixed.reshape(seq_rows, width).astype(jnp.bfloat16)


def shards_any(tokens, gain, w_qkv, w_out, cache_keys, cache_values, cache_lengths):
    seq_rows = tokens.shape[0]
    groups = lax.axis_size("gx")
    blocks = lax.axis_size("yz")
    width = w_out.shape[0] * blocks
    xf = tokens.astype(jnp.float32)
    mean = jnp.mean(xf, axis=1, keepdims=True)
    centered = xf - mean
    variance = jnp.mean(centered * centered, axis=1, keepdims=True)
    normed = (centered / jnp.sqrt(variance + 1e-05) * gain[None, :]).astype(jnp.bfloat16)
    feature_rows = lax.all_to_all(normed, "gx", split_axis=1, concat_axis=0, tiled=True)
    column_count = w_qkv.shape[1]
    partial_value = jnp.dot(
        lax.all_gather(feature_rows, "yz", axis=0, tiled=True),
        w_qkv,
        preferred_element_type=jnp.float32,
    )
    partial_value = partial_value.reshape(blocks, groups, seq_rows, column_count)
    summed = lax.psum_scatter(partial_value, "gx", scatter_dimension=1, tiled=True)
    summed = summed.reshape(blocks, seq_rows, column_count).astype(jnp.bfloat16)
    received = lax.all_to_all(summed, "yz", split_axis=0, concat_axis=0, tiled=True)
    qkv = received.transpose(1, 0, 2).reshape(seq_rows, blocks * column_count)
    attended = attend_local(qkv, cache_keys, cache_values, cache_lengths, width)
    feature_block = w_out.shape[0]
    split = attended.reshape(seq_rows, blocks, feature_block)
    received = lax.all_to_all(split, "yz", split_axis=1, concat_axis=0, tiled=True)
    received = received.reshape(blocks * seq_rows, feature_block)
    everyone = lax.all_gather(received, "gx", axis=0, tiled=True)
    everyone = everyone.reshape(groups, blocks * seq_rows, feature_block)
    summed = lax.psum_scatter(
        jnp.einsum("gcf,fd->cgd", everyone, w_out, preferred_element_type=jnp.float32),
        "yz",
        scatter_dimension=0,
        tiled=True,
    )
    return summed.transpose(1, 0, 2).astype(jnp.bfloat16)


def solution(mesh):
    placed = (
        P(("parts", "gx", "yz"), None),
        P(),
        P("gx", "yz"),
        P("yz", "gx"),
        P(("parts", "gx", "yz"), None, None),
        P(("parts", "gx", "yz"), None, None),
        P(("parts", "gx", "yz")),
    )
    small = mesh.shape["gx"] == 4 and mesh.shape["yz"] == 4
    return jax.shard_map(
        shards if small else shards_any,
        mesh=mesh,
        in_specs=placed,
        out_specs=P(None, ("parts", "yz"), "gx"),
        check_vma=False,
    )
```

```python
import functools

import jax
import jax.numpy as jnp
from jax import lax
from jax.experimental import pallas as pl
from jax.experimental.pallas import tpu as pltpu
from jax.sharding import PartitionSpec as P

VMEM = pl.BlockSpec(memory_space=pltpu.VMEM)
SMEM = pl.BlockSpec(memory_space=pltpu.SMEM)
ANY = pl.BlockSpec(memory_space=pl.ANY)
MIB = 1 << 20
A1 = (0, 1, 3, 2)
A2 = (0, 1, 2, 3, 4, 5)
B1 = (0, 1, 2)
WIDE = jnp.float32
B2 = (0, 2, 3, 1)
C1 = (0, 3, 2, 1)
C2 = (0, 1, 2, 3)
D = (0, 2, 1, 3)


def call(body, outs, in_specs, args, limit=8, scratch=(), flops=0, traffic=0, order=()):
    order = [*order, *range(len(order), len(args))]

    def ordered(*refs):
        ins = [refs[order.index(i)] for i in range(len(args))]
        body(*ins, *refs[len(args) :])

    return pl.pallas_call(
        ordered,
        out_shape=outs,
        in_specs=[in_specs[i] for i in order],
        out_specs=jax.tree.map(lambda _: VMEM, outs),
        scratch_shapes=scratch,
        compiler_params=pltpu.CompilerParams(vmem_limit_bytes=limit * MIB),
        cost_estimate=pl.CostEstimate(flops=flops, bytes_accessed=traffic, transcendentals=0),
    )(*[args[i] for i in order])


def near(x):
    return pltpu.with_memory_space_constraint(x, pltpu.VMEM)


def far(x):
    return pltpu.with_memory_space_constraint(x, pltpu.HBM)


def struct(shape, dtype=jnp.bfloat16):
    return jax.ShapeDtypeStruct(shape, dtype)


def exchange(pieces, axis):
    size = lax.axis_size(axis)
    return [pieces[0]] + [
        lax.ppermute(pieces[k], axis, [(i, i ^ k) for i in range(size)]) for k in range(1, size)
    ]


def swap(piece, axis, k):
    return lax.ppermute(piece, axis, [(i, i ^ k) for i in range(lax.axis_size(axis))])


def norm_body(x_hbm, gain_hbm, *refs):
    *out_refs, x_ref, gain_ref, sems = refs
    copies = [
        pltpu.make_async_copy(x_hbm, x_ref, sems.at[0]),
        pltpu.make_async_copy(gain_hbm, gain_ref, sems.at[1]),
    ]
    for copy in copies:
        copy.start()
    block = out_refs[0].shape[1]
    me = lax.axis_index("gx")
    copies[0].wait()
    x = x_ref[...].astype(jnp.float32)
    mean = jnp.mean(x, axis=1, keepdims=True)
    centered = x - mean
    variance = jnp.mean(centered * centered, axis=1, keepdims=True)
    inverse = 1.0 / jnp.sqrt(variance + 1e-05)
    copies[1].wait()
    for k, out_ref in enumerate(out_refs):
        columns = pl.ds(pl.multiple_of((me ^ k) * block, 128), block)
        part = x_ref[:, columns].astype(jnp.float32) - mean
        out_ref[...] = (part * inverse * gain_ref[:, columns]).astype(jnp.bfloat16)


def regroup(total, n):
    each = total.shape[0] // (n * n)
    return [
        jnp.concatenate(
            [total[(j * n + k) * each : (j * n + k + 1) * each] for j in range(n)], axis=0
        )
        for k in range(n)
    ]


def dot_body(cuts, *refs):
    refs = list(refs)
    pieces = [jnp.concatenate([refs.pop(0)[...] for _ in range(n)], axis=1) for n in cuts]
    w_ref, *outs = refs
    rows = jnp.concatenate(pieces, axis=0)
    size = rows.shape[1] // max(cuts)
    total = sum(
        jnp.dot(rows[:, at : at + size], w_ref[at : at + size], preferred_element_type=jnp.float32)
        for at in range(0, rows.shape[1], size)
    )
    for group, out in zip(regroup(total, len(cuts)), outs):
        out[...] = group.astype(out.dtype)


def dot(pieces, w, kept=(0,), order=()):
    n, rows, (depth, width) = len(pieces), pieces[0][0].shape[0], w.shape
    outs = [struct((rows, width), jnp.float32 if k in kept else jnp.bfloat16) for k in range(n)]
    ins = [part for piece in pieces for part in piece]
    return call(
        functools.partial(dot_body, [len(piece) for piece in pieces]),
        outs,
        [VMEM] * (len(ins) + 1),
        [*ins, near(w)],
        limit=6,
        flops=2 * n * rows * depth * width,
        traffic=2 * depth * width,
        order=order,
    )


def add_body(kept, received, out):
    out[...] = (kept[...] + received[...]).astype(out.dtype)


def total_body(*refs):
    ins, outs = refs[:3], refs[3:]
    total = ins[0][...]
    for r in ins[1:]:
        total = total + r[...].astype(jnp.float32)
    each = outs[0].shape[0]
    for j, out in enumerate(outs):
        out[...] = total[j * each : (j + 1) * each].astype(jnp.bfloat16)


def attend_body(blocks, heads, *refs):
    pieces, (key_ref, value_ref, length_ref) = refs[:blocks], refs[blocks : blocks + 3]
    outs = refs[blocks + 3 : 2 * blocks + 3]
    row_ref, query_ref, mixed_ref = refs[2 * blocks + 3 :]
    me = lax.axis_index("yz")
    part = pieces[0].shape[1]
    seqs, slots, head = key_ref.shape
    scale = 1.0 / jnp.sqrt(jnp.float32(head))
    for j, piece in enumerate(pieces):
        row_ref[:, pl.ds(pl.multiple_of((me ^ j) * part, 128), part)] = piece[...].astype(jnp.float32)
    for h in range(heads):
        query_ref[h] = row_ref[:, h * head : (h + 1) * head]
    slot = lax.broadcasted_iota(jnp.int32, (1, slots), 1)
    width = heads * head
    queries = [query_ref[:, s, :] for s in range(seqs)]
    owns = [
        jnp.sum(queries[s] * row_ref[s : s + 1, width : width + head], axis=1, keepdims=True) * scale
        for s in range(seqs)
    ]
    scores = [
        lax.dot_general(
            queries[s].astype(jnp.bfloat16),
            key_ref[s],
            (((1,), (1,)), ((), ())),
            preferred_element_type=jnp.float32,
        )
        for s in range(seqs)
    ]
    masked = [jnp.where(slot < length_ref[s], scores[s] * scale, -jnp.inf) for s in range(seqs)]
    tops = [jnp.maximum(jnp.max(masked[s], axis=1, keepdims=True), owns[s]) for s in range(seqs)]
    weights = [jnp.exp(masked[s] - tops[s]) for s in range(seqs)]
    own_weights = [jnp.exp(owns[s] - tops[s]) for s in range(seqs)]
    totals = [jnp.sum(weights[s], axis=1, keepdims=True) + own_weights[s] for s in range(seqs)]
    probs = [(weights[s] / totals[s]).astype(jnp.bfloat16) for s in range(seqs)]
    mixed = [
        jnp.dot(probs[s], value_ref[s], preferred_element_type=jnp.float32) for s in range(seqs)
    ]
    for s in range(seqs):
        own_prob = (own_weights[s] / totals[s]).astype(jnp.bfloat16).astype(jnp.float32)
        value_new = row_ref[s : s + 1, width + head : width + 2 * head]
        mixed_ref[:, s, :] = mixed[s] + own_prob * value_new
    each = heads // blocks
    for j, out in enumerate(outs):
        first = (me ^ j) * each
        for h in range(each):
            out[:, h * head : (h + 1) * head] = mixed_ref[first + h].astype(jnp.bfloat16)


def attend(pieces, cache_keys, cache_values, cache_lengths, width):
    seqs, slots, head = cache_keys.shape
    blocks, heads = len(pieces), width // head
    keys = pltpu.with_memory_space_constraint(cache_keys, pltpu.VMEM)
    values = pltpu.with_memory_space_constraint(cache_values, pltpu.VMEM)
    return call(
        functools.partial(attend_body, blocks, heads),
        [struct((seqs, width // blocks))] * blocks,
        [VMEM] * (blocks + 2) + [SMEM],
        [*pieces, keys, values, cache_lengths],
        order=B2,
        limit=12,
        scratch=[
            pltpu.VMEM((seqs, width + 2 * head), jnp.float32),
            pltpu.VMEM((heads, seqs, head), jnp.float32),
            pltpu.VMEM((heads, seqs, head), jnp.float32),
        ],
        flops=50_000_000_000,
        traffic=4 * seqs * slots * head,
    )


def cut_body(*refs):
    rows = jnp.concatenate([r[...] for r in refs[:4]], axis=0)
    whole, early, late = refs[4:]
    whole[...] = rows
    early[...] = rows[:, : early.shape[1]]
    late[...] = rows[:, early.shape[1] :]


def join_body(*refs):
    refs[-1][...] = jnp.concatenate([r[...] for r in refs[:-1]], axis=0)


def place_body(n, *refs):
    pieces, out_ref = refs[:n], refs[n]
    me = lax.axis_index("gx")
    total = pieces[0][...]
    for p in pieces[1:]:
        total = total + p[...].astype(jnp.float32)
    each = out_ref.shape[1]
    for k in range(out_ref.shape[0]):
        out_ref[me ^ k] = total[k * each : (k + 1) * each].astype(jnp.bfloat16)


def shards(tokens, gain, w_qkv, w_out, cache_keys, cache_values, cache_lengths):
    groups, blocks = lax.axis_size("gx"), lax.axis_size("yz")
    seqs, depth = tokens.shape[0], w_qkv.shape[0]
    width = w_out.shape[0] * blocks
    normed = call(
        norm_body,
        [struct((seqs, depth))] * groups,
        [ANY, ANY],
        [far(tokens), far(gain.reshape(1, -1))],
        scratch=[
            pltpu.VMEM(tokens.shape, tokens.dtype),
            pltpu.VMEM((1, gain.shape[0]), gain.dtype),
            pltpu.SemaphoreType.DMA((2,)),
        ],
        flops=50_000_000_000,
    )
    half = depth // 2
    mine, *halves = call(
        cut_body,
        [struct((groups * seqs, size)) for size in (depth, half, half)],
        [VMEM] * groups,
        exchange(normed, "gx"),
        order=A1,
    )
    one = swap(mine, "yz", 1)
    two = [swap(part, "yz", 2) for part in halves]
    three = [swap(part, "yz", 1) for part in two]
    own, one, two, three = dot([[mine], [one], two, three], w_qkv, kept=(0, 1, 2, 3), order=A2)
    two = call(add_body, struct(two.shape, WIDE), [VMEM] * 2, [two, swap(three, "gx", 1)])
    parts = call(
        total_body,
        [struct((seqs, w_qkv.shape[1]))] * blocks,
        [VMEM] * 3,
        [own, swap(two, "gx", 2), swap(one, "gx", 1)],
        order=B1,
    )
    attended = attend(exchange(parts, "yz"), cache_keys, cache_values, cache_lengths, width)
    got = exchange(attended, "yz")
    mine = call(join_body, struct((4 * seqs, got[0].shape[1])), [VMEM] * 4, got, flops=50_000_000_000, order=C1)
    two = swap(mine, "gx", 2)
    pieces = [[mine], [swap(mine, "gx", 1)], [two], [swap(two, "gx", 1)]]
    sums = exchange(dot(pieces, w_out, order=C2), "yz")
    return call(
        functools.partial(place_body, blocks),
        struct((groups, seqs, w_out.shape[1])),
        [VMEM] * blocks,
        sums,
        order=D,
    )


def attend_local(qkv, cache_keys, cache_values, cache_lengths, width):
    seq_rows = qkv.shape[0]
    head = cache_keys.shape[2]
    slots = cache_keys.shape[1]
    scale = 1.0 / jnp.sqrt(jnp.float32(head))
    query = qkv[:, :width].reshape(seq_rows, width // head, head)
    key_new = qkv[:, width : width + head]
    value_new = qkv[:, width + head :]
    scores = (
        jnp.einsum("shd,std->sht", query, cache_keys, preferred_element_type=jnp.float32) * scale
    )
    own = jnp.einsum("shd,sd->sh", query, key_new, preferred_element_type=jnp.float32) * scale
    valid = jnp.arange(slots, dtype=jnp.int32)[None, None, :] < cache_lengths[:, None, None]
    masked = jnp.where(valid, scores, -jnp.inf)
    top = jnp.maximum(jnp.max(masked, axis=2), own)
    weights = jnp.where(valid, jnp.exp(masked - top[:, :, None]), 0.0)
    own_weight = jnp.exp(own - top)
    total = jnp.sum(weights, axis=2) + own_weight
    probs = (weights / total[:, :, None]).astype(jnp.bfloat16)
    own_prob = (own_weight / total).astype(jnp.bfloat16)
    mixed = jnp.einsum("sht,std->shd", probs, cache_values, preferred_element_type=jnp.float32)
    mixed = (
        mixed + own_prob.astype(jnp.float32)[:, :, None] * value_new.astype(jnp.float32)[:, None, :]
    )
    return mixed.reshape(seq_rows, width).astype(jnp.bfloat16)


def shards_any(tokens, gain, w_qkv, w_out, cache_keys, cache_values, cache_lengths):
    seq_rows = tokens.shape[0]
    groups = lax.axis_size("gx")
    blocks = lax.axis_size("yz")
    width = w_out.shape[0] * blocks
    xf = tokens.astype(jnp.float32)
    mean = jnp.mean(xf, axis=1, keepdims=True)
    centered = xf - mean
    variance = jnp.mean(centered * centered, axis=1, keepdims=True)
    normed = (centered / jnp.sqrt(variance + 1e-05) * gain[None, :]).astype(jnp.bfloat16)
    feature_rows = lax.all_to_all(normed, "gx", split_axis=1, concat_axis=0, tiled=True)
    column_count = w_qkv.shape[1]
    partial_value = jnp.dot(
        lax.all_gather(feature_rows, "yz", axis=0, tiled=True),
        w_qkv,
        preferred_element_type=jnp.float32,
    )
    partial_value = partial_value.reshape(blocks, groups, seq_rows, column_count)
    summed = lax.psum_scatter(partial_value, "gx", scatter_dimension=1, tiled=True)
    summed = summed.reshape(blocks, seq_rows, column_count).astype(jnp.bfloat16)
    received = lax.all_to_all(summed, "yz", split_axis=0, concat_axis=0, tiled=True)
    qkv = received.transpose(1, 0, 2).reshape(seq_rows, blocks * column_count)
    attended = attend_local(qkv, cache_keys, cache_values, cache_lengths, width)
    feature_block = w_out.shape[0]
    split = attended.reshape(seq_rows, blocks, feature_block)
    received = lax.all_to_all(split, "yz", split_axis=1, concat_axis=0, tiled=True)
    received = received.reshape(blocks * seq_rows, feature_block)
    everyone = lax.all_gather(received, "gx", axis=0, tiled=True)
    everyone = everyone.reshape(groups, blocks * seq_rows, feature_block)
    summed = lax.psum_scatter(
        jnp.einsum("gcf,fd->cgd", everyone, w_out, preferred_element_type=jnp.float32),
        "yz",
        scatter_dimension=0,
        tiled=True,
    )
    return summed.transpose(1, 0, 2).astype(jnp.bfloat16)


def solution(mesh):
    placed = (
        P(("parts", "gx", "yz"), None),
        P(),
        P("gx", "yz"),
        P("yz", "gx"),
        P(("parts", "gx", "yz"), None, None),
        P(("parts", "gx", "yz"), None, None),
        P(("parts", "gx", "yz")),
    )
    small = mesh.shape["gx"] == 4 and mesh.shape["yz"] == 4
    return jax.shard_map(
        shards if small else shards_any,
        mesh=mesh,
        in_specs=placed,
        out_specs=P(None, ("parts", "yz"), "gx"),
        check_vma=False,
    )
```

```python
import functools

import jax
import jax.numpy as jnp
from jax import lax
from jax.experimental import pallas as pl
from jax.experimental.pallas import tpu as pltpu
from jax.sharding import PartitionSpec as P

VMEM = pl.BlockSpec(memory_space=pltpu.VMEM)
SMEM = pl.BlockSpec(memory_space=pltpu.SMEM)
ANY = pl.BlockSpec(memory_space=pl.ANY)
MIB = 1 << 20
A1 = (0, 1, 3, 2)
A2 = (0, 1, 2, 3, 4, 5)
B1 = (0, 1, 2)
WIDE = jnp.float32
B2 = (0, 2, 3, 1)
C1 = (0, 2, 3, 1)
C2 = (0, 1, 2, 3)
D = (0, 2, 1, 3)


def call(body, outs, in_specs, args, limit=8, scratch=(), flops=0, traffic=0, order=()):
    order = [*order, *range(len(order), len(args))]

    def ordered(*refs):
        ins = [refs[order.index(i)] for i in range(len(args))]
        body(*ins, *refs[len(args) :])

    return pl.pallas_call(
        ordered,
        out_shape=outs,
        in_specs=[in_specs[i] for i in order],
        out_specs=jax.tree.map(lambda _: VMEM, outs),
        scratch_shapes=scratch,
        compiler_params=pltpu.CompilerParams(vmem_limit_bytes=limit * MIB),
        cost_estimate=pl.CostEstimate(flops=flops, bytes_accessed=traffic, transcendentals=0),
    )(*[args[i] for i in order])


def near(x):
    return pltpu.with_memory_space_constraint(x, pltpu.VMEM)


def far(x):
    return pltpu.with_memory_space_constraint(x, pltpu.HBM)


def struct(shape, dtype=jnp.bfloat16):
    return jax.ShapeDtypeStruct(shape, dtype)


def exchange(pieces, axis):
    size = lax.axis_size(axis)
    return [pieces[0]] + [
        lax.ppermute(pieces[k], axis, [(i, i ^ k) for i in range(size)]) for k in range(1, size)
    ]


def swap(piece, axis, k):
    return lax.ppermute(piece, axis, [(i, i ^ k) for i in range(lax.axis_size(axis))])


def norm_body(x_hbm, gain_hbm, *refs):
    *out_refs, x_ref, gain_ref, sems = refs
    copies = [
        pltpu.make_async_copy(x_hbm, x_ref, sems.at[0]),
        pltpu.make_async_copy(gain_hbm, gain_ref, sems.at[1]),
    ]
    for copy in copies:
        copy.start()
    block = out_refs[0].shape[1]
    me = lax.axis_index("gx")
    copies[0].wait()
    x = x_ref[...].astype(jnp.float32)
    mean = jnp.mean(x, axis=1, keepdims=True)
    centered = x - mean
    variance = jnp.mean(centered * centered, axis=1, keepdims=True)
    inverse = 1.0 / jnp.sqrt(variance + 1e-05)
    copies[1].wait()
    for k, out_ref in enumerate(out_refs):
        columns = pl.ds(pl.multiple_of((me ^ k) * block, 128), block)
        part = x_ref[:, columns].astype(jnp.float32) - mean
        out_ref[...] = (part * inverse * gain_ref[:, columns]).astype(jnp.bfloat16)


def regroup(total, n):
    each = total.shape[0] // (n * n)
    return [
        jnp.concatenate(
            [total[(j * n + k) * each : (j * n + k + 1) * each] for j in range(n)], axis=0
        )
        for k in range(n)
    ]


def dot_body(cuts, *refs):
    refs = list(refs)
    pieces = [jnp.concatenate([refs.pop(0)[...] for _ in range(n)], axis=1) for n in cuts]
    w_ref, *outs = refs
    rows = jnp.concatenate(pieces, axis=0)
    size = rows.shape[1] // max(cuts)
    total = sum(
        jnp.dot(rows[:, at : at + size], w_ref[at : at + size], preferred_element_type=jnp.float32)
        for at in range(0, rows.shape[1], size)
    )
    for group, out in zip(regroup(total, len(cuts)), outs):
        out[...] = group.astype(out.dtype)


def dot(pieces, w, kept=(0,), order=()):
    n, rows, (depth, width) = len(pieces), pieces[0][0].shape[0], w.shape
    outs = [struct((rows, width), jnp.float32 if k in kept else jnp.bfloat16) for k in range(n)]
    ins = [part for piece in pieces for part in piece]
    return call(
        functools.partial(dot_body, [len(piece) for piece in pieces]),
        outs,
        [VMEM] * (len(ins) + 1),
        [*ins, near(w)],
        limit=6,
        flops=2 * n * rows * depth * width,
        traffic=2 * depth * width,
        order=order,
    )


def add_body(kept, received, out):
    out[...] = (kept[...] + received[...]).astype(out.dtype)


def total_body(*refs):
    ins, outs = refs[:3], refs[3:]
    total = ins[0][...]
    for r in ins[1:]:
        total = total + r[...].astype(jnp.float32)
    each = outs[0].shape[0]
    for j, out in enumerate(outs):
        out[...] = total[j * each : (j + 1) * each].astype(jnp.bfloat16)


def attend_body(blocks, heads, *refs):
    pieces, (key_ref, value_ref, length_ref) = refs[:blocks], refs[blocks : blocks + 3]
    outs = refs[blocks + 3 : 2 * blocks + 3]
    row_ref, query_ref, mixed_ref = refs[2 * blocks + 3 :]
    me = lax.axis_index("yz")
    part = pieces[0].shape[1]
    seqs, slots, head = key_ref.shape
    scale = 1.0 / jnp.sqrt(jnp.float32(head))
    for j, piece in enumerate(pieces):
        row_ref[:, pl.ds(pl.multiple_of((me ^ j) * part, 128), part)] = piece[...].astype(jnp.float32)
    for h in range(heads):
        query_ref[h] = row_ref[:, h * head : (h + 1) * head]
    slot = lax.broadcasted_iota(jnp.int32, (1, slots), 1)
    width = heads * head
    queries = [query_ref[:, s, :] for s in range(seqs)]
    owns = [
        jnp.sum(queries[s] * row_ref[s : s + 1, width : width + head], axis=1, keepdims=True) * scale
        for s in range(seqs)
    ]
    scores = [
        lax.dot_general(
            queries[s].astype(jnp.bfloat16),
            key_ref[s],
            (((1,), (1,)), ((), ())),
            preferred_element_type=jnp.float32,
        )
        for s in range(seqs)
    ]
    masked = [jnp.where(slot < length_ref[s], scores[s] * scale, -jnp.inf) for s in range(seqs)]
    tops = [jnp.maximum(jnp.max(masked[s], axis=1, keepdims=True), owns[s]) for s in range(seqs)]
    weights = [jnp.exp(masked[s] - tops[s]) for s in range(seqs)]
    own_weights = [jnp.exp(owns[s] - tops[s]) for s in range(seqs)]
    totals = [jnp.sum(weights[s], axis=1, keepdims=True) + own_weights[s] for s in range(seqs)]
    probs = [(weights[s] / totals[s]).astype(jnp.bfloat16) for s in range(seqs)]
    mixed = [
        jnp.dot(probs[s], value_ref[s], preferred_element_type=jnp.float32) for s in range(seqs)
    ]
    for s in range(seqs):
        own_prob = (own_weights[s] / totals[s]).astype(jnp.bfloat16).astype(jnp.float32)
        value_new = row_ref[s : s + 1, width + head : width + 2 * head]
        mixed_ref[:, s, :] = mixed[s] + own_prob * value_new
    each = heads // blocks
    for j, out in enumerate(outs):
        first = (me ^ j) * each
        for h in range(each):
            out[:, h * head : (h + 1) * head] = mixed_ref[first + h].astype(jnp.bfloat16)


def attend(pieces, cache_keys, cache_values, cache_lengths, width):
    seqs, slots, head = cache_keys.shape
    blocks, heads = len(pieces), width // head
    keys = pltpu.with_memory_space_constraint(cache_keys, pltpu.VMEM)
    values = pltpu.with_memory_space_constraint(cache_values, pltpu.VMEM)
    return call(
        functools.partial(attend_body, blocks, heads),
        [struct((seqs, width // blocks))] * blocks,
        [VMEM] * (blocks + 2) + [SMEM],
        [*pieces, keys, values, cache_lengths],
        order=B2,
        limit=12,
        scratch=[
            pltpu.VMEM((seqs, width + 2 * head), jnp.float32),
            pltpu.VMEM((heads, seqs, head), jnp.float32),
            pltpu.VMEM((heads, seqs, head), jnp.float32),
        ],
        flops=50_000_000_000,
        traffic=4 * seqs * slots * head,
    )


def cut_body(*refs):
    rows = jnp.concatenate([r[...] for r in refs[:4]], axis=0)
    whole, early, late = refs[4:]
    whole[...] = rows
    early[...] = rows[:, : early.shape[1]]
    late[...] = rows[:, early.shape[1] :]


def join_body(*refs):
    refs[-1][...] = jnp.concatenate([r[...] for r in refs[:-1]], axis=0)


def place_body(n, *refs):
    pieces, out_ref = refs[:n], refs[n]
    me = lax.axis_index("gx")
    total = pieces[0][...]
    for p in pieces[1:]:
        total = total + p[...].astype(jnp.float32)
    each = out_ref.shape[1]
    for k in range(out_ref.shape[0]):
        out_ref[me ^ k] = total[k * each : (k + 1) * each].astype(jnp.bfloat16)


def shards(tokens, gain, w_qkv, w_out, cache_keys, cache_values, cache_lengths):
    groups, blocks = lax.axis_size("gx"), lax.axis_size("yz")
    seqs, depth = tokens.shape[0], w_qkv.shape[0]
    width = w_out.shape[0] * blocks
    normed = call(
        norm_body,
        [struct((seqs, depth))] * groups,
        [ANY, ANY],
        [far(tokens), far(gain.reshape(1, -1))],
        scratch=[
            pltpu.VMEM(tokens.shape, tokens.dtype),
            pltpu.VMEM((1, gain.shape[0]), gain.dtype),
            pltpu.SemaphoreType.DMA((2,)),
        ],
        flops=50_000_000_000,
    )
    half = depth // 2
    mine, *halves = call(
        cut_body,
        [struct((groups * seqs, size)) for size in (depth, half, half)],
        [VMEM] * groups,
        exchange(normed, "gx"),
        order=A1,
    )
    one = swap(mine, "yz", 1)
    two = [swap(part, "yz", 2) for part in halves]
    three = [swap(part, "yz", 1) for part in two]
    own, one, two, three = dot([[mine], [one], two, three], w_qkv, kept=(0, 1, 2, 3), order=A2)
    two = call(add_body, struct(two.shape, WIDE), [VMEM] * 2, [two, swap(three, "gx", 1)])
    parts = call(
        total_body,
        [struct((seqs, w_qkv.shape[1]))] * blocks,
        [VMEM] * 3,
        [own, swap(two, "gx", 2), swap(one, "gx", 1)],
        order=B1,
    )
    attended = attend(exchange(parts, "yz"), cache_keys, cache_values, cache_lengths, width)
    got = exchange(attended, "yz")
    mine = call(join_body, struct((4 * seqs, got[0].shape[1])), [VMEM] * 4, got, flops=50_000_000_000, order=C1)
    two = swap(mine, "gx", 2)
    pieces = [[mine], [swap(mine, "gx", 1)], [two], [swap(two, "gx", 1)]]
    sums = exchange(dot(pieces, w_out, order=C2), "yz")
    return call(
        functools.partial(place_body, blocks),
        struct((groups, seqs, w_out.shape[1])),
        [VMEM] * blocks,
        sums,
        order=D,
    )


def attend_local(qkv, cache_keys, cache_values, cache_lengths, width):
    seq_rows = qkv.shape[0]
    head = cache_keys.shape[2]
    slots = cache_keys.shape[1]
    scale = 1.0 / jnp.sqrt(jnp.float32(head))
    query = qkv[:, :width].reshape(seq_rows, width // head, head)
    key_new = qkv[:, width : width + head]
    value_new = qkv[:, width + head :]
    scores = (
        jnp.einsum("shd,std->sht", query, cache_keys, preferred_element_type=jnp.float32) * scale
    )
    own = jnp.einsum("shd,sd->sh", query, key_new, preferred_element_type=jnp.float32) * scale
    valid = jnp.arange(slots, dtype=jnp.int32)[None, None, :] < cache_lengths[:, None, None]
    masked = jnp.where(valid, scores, -jnp.inf)
    top = jnp.maximum(jnp.max(masked, axis=2), own)
    weights = jnp.where(valid, jnp.exp(masked - top[:, :, None]), 0.0)
    own_weight = jnp.exp(own - top)
    total = jnp.sum(weights, axis=2) + own_weight
    probs = (weights / total[:, :, None]).astype(jnp.bfloat16)
    own_prob = (own_weight / total).astype(jnp.bfloat16)
    mixed = jnp.einsum("sht,std->shd", probs, cache_values, preferred_element_type=jnp.float32)
    mixed = (
        mixed + own_prob.astype(jnp.float32)[:, :, None] * value_new.astype(jnp.float32)[:, None, :]
    )
    return mixed.reshape(seq_rows, width).astype(jnp.bfloat16)


def shards_any(tokens, gain, w_qkv, w_out, cache_keys, cache_values, cache_lengths):
    seq_rows = tokens.shape[0]
    groups = lax.axis_size("gx")
    blocks = lax.axis_size("yz")
    width = w_out.shape[0] * blocks
    xf = tokens.astype(jnp.float32)
    mean = jnp.mean(xf, axis=1, keepdims=True)
    centered = xf - mean
    variance = jnp.mean(centered * centered, axis=1, keepdims=True)
    normed = (centered / jnp.sqrt(variance + 1e-05) * gain[None, :]).astype(jnp.bfloat16)
    feature_rows = lax.all_to_all(normed, "gx", split_axis=1, concat_axis=0, tiled=True)
    column_count = w_qkv.shape[1]
    partial_value = jnp.dot(
        lax.all_gather(feature_rows, "yz", axis=0, tiled=True),
        w_qkv,
        preferred_element_type=jnp.float32,
    )
    partial_value = partial_value.reshape(blocks, groups, seq_rows, column_count)
    summed = lax.psum_scatter(partial_value, "gx", scatter_dimension=1, tiled=True)
    summed = summed.reshape(blocks, seq_rows, column_count).astype(jnp.bfloat16)
    received = lax.all_to_all(summed, "yz", split_axis=0, concat_axis=0, tiled=True)
    qkv = received.transpose(1, 0, 2).reshape(seq_rows, blocks * column_count)
    attended = attend_local(qkv, cache_keys, cache_values, cache_lengths, width)
    feature_block = w_out.shape[0]
    split = attended.reshape(seq_rows, blocks, feature_block)
    received = lax.all_to_all(split, "yz", split_axis=1, concat_axis=0, tiled=True)
    received = received.reshape(blocks * seq_rows, feature_block)
    everyone = lax.all_gather(received, "gx", axis=0, tiled=True)
    everyone = everyone.reshape(groups, blocks * seq_rows, feature_block)
    summed = lax.psum_scatter(
        jnp.einsum("gcf,fd->cgd", everyone, w_out, preferred_element_type=jnp.float32),
        "yz",
        scatter_dimension=0,
        tiled=True,
    )
    return summed.transpose(1, 0, 2).astype(jnp.bfloat16)


def solution(mesh):
    placed = (
        P(("parts", "gx", "yz"), None),
        P(),
        P("gx", "yz"),
        P("yz", "gx"),
        P(("parts", "gx", "yz"), None, None),
        P(("parts", "gx", "yz"), None, None),
        P(("parts", "gx", "yz")),
    )
    small = mesh.shape["gx"] == 4 and mesh.shape["yz"] == 4
    return jax.shard_map(
        shards if small else shards_any,
        mesh=mesh,
        in_specs=placed,
        out_specs=P(None, ("parts", "yz"), "gx"),
        check_vma=False,
    )
```

```python
import functools

import jax
import jax.numpy as jnp
from jax import lax
from jax.experimental import pallas as pl
from jax.experimental.pallas import tpu as pltpu
from jax.sharding import PartitionSpec as P

VMEM = pl.BlockSpec(memory_space=pltpu.VMEM)
SMEM = pl.BlockSpec(memory_space=pltpu.SMEM)
ANY = pl.BlockSpec(memory_space=pl.ANY)
MIB = 1 << 20
A1 = (0, 1, 3, 2)
A2 = (0, 1, 2, 3, 4, 5)
B1 = (0, 1, 2)
WIDE = jnp.float32
B2 = (0, 2, 3, 1)
C1 = (0, 2, 3, 1)
C2 = (0, 1, 2, 3)
D = (0, 2, 1, 3)


def call(body, outs, in_specs, args, limit=8, scratch=(), flops=0, traffic=0, order=()):
    order = [*order, *range(len(order), len(args))]

    def ordered(*refs):
        ins = [refs[order.index(i)] for i in range(len(args))]
        body(*ins, *refs[len(args) :])

    return pl.pallas_call(
        ordered,
        out_shape=outs,
        in_specs=[in_specs[i] for i in order],
        out_specs=jax.tree.map(lambda _: VMEM, outs),
        scratch_shapes=scratch,
        compiler_params=pltpu.CompilerParams(vmem_limit_bytes=limit * MIB),
        cost_estimate=pl.CostEstimate(flops=flops, bytes_accessed=traffic, transcendentals=0),
    )(*[args[i] for i in order])


def near(x):
    return pltpu.with_memory_space_constraint(x, pltpu.VMEM)


def far(x):
    return pltpu.with_memory_space_constraint(x, pltpu.HBM)


def struct(shape, dtype=jnp.bfloat16):
    return jax.ShapeDtypeStruct(shape, dtype)


def exchange(pieces, axis):
    size = lax.axis_size(axis)
    return [pieces[0]] + [
        lax.ppermute(pieces[k], axis, [(i, i ^ k) for i in range(size)]) for k in range(1, size)
    ]


def swap(piece, axis, k):
    return lax.ppermute(piece, axis, [(i, i ^ k) for i in range(lax.axis_size(axis))])


def norm_body(x_hbm, gain_hbm, *refs):
    *out_refs, x_ref, gain_ref, sems = refs
    copies = [
        pltpu.make_async_copy(x_hbm, x_ref, sems.at[0]),
        pltpu.make_async_copy(gain_hbm, gain_ref, sems.at[1]),
    ]
    for copy in copies:
        copy.start()
    block = out_refs[0].shape[1]
    me = lax.axis_index("gx")
    copies[0].wait()
    x = x_ref[...].astype(jnp.float32)
    mean = jnp.mean(x, axis=1, keepdims=True)
    centered = x - mean
    variance = jnp.mean(centered * centered, axis=1, keepdims=True)
    inverse = 1.0 / jnp.sqrt(variance + 1e-05)
    copies[1].wait()
    for k, out_ref in enumerate(out_refs):
        columns = pl.ds(pl.multiple_of((me ^ k) * block, 128), block)
        part = x_ref[:, columns].astype(jnp.float32) - mean
        out_ref[...] = (part * inverse * gain_ref[:, columns]).astype(jnp.bfloat16)


def regroup(total, n):
    each = total.shape[0] // (n * n)
    return [
        jnp.concatenate(
            [total[(j * n + k) * each : (j * n + k + 1) * each] for j in range(n)], axis=0
        )
        for k in range(n)
    ]


def dot_body(cuts, *refs):
    refs = list(refs)
    pieces = [jnp.concatenate([refs.pop(0)[...] for _ in range(n)], axis=1) for n in cuts]
    w_ref, *outs = refs
    rows = jnp.concatenate(pieces, axis=0)
    size = rows.shape[1] // max(cuts)
    total = sum(
        jnp.dot(rows[:, at : at + size], w_ref[at : at + size], preferred_element_type=jnp.float32)
        for at in range(0, rows.shape[1], size)
    )
    for group, out in zip(regroup(total, len(cuts)), outs):
        out[...] = group.astype(out.dtype)


def dot(pieces, w, kept=(0,), order=()):
    n, rows, (depth, width) = len(pieces), pieces[0][0].shape[0], w.shape
    outs = [struct((rows, width), jnp.float32 if k in kept else jnp.bfloat16) for k in range(n)]
    ins = [part for piece in pieces for part in piece]
    return call(
        functools.partial(dot_body, [len(piece) for piece in pieces]),
        outs,
        [VMEM] * (len(ins) + 1),
        [*ins, near(w)],
        limit=6,
        flops=2 * n * rows * depth * width,
        traffic=2 * depth * width,
        order=order,
    )


def add_body(kept, received, out):
    out[...] = (kept[...] + received[...]).astype(out.dtype)


def total_body(*refs):
    ins, outs = refs[:3], refs[3:]
    total = ins[0][...]
    for r in ins[1:]:
        total = total + r[...].astype(jnp.float32)
    each = outs[0].shape[0]
    for j, out in enumerate(outs):
        out[...] = total[j * each : (j + 1) * each].astype(jnp.bfloat16)


def turn_body(key_ref, out_ref):
    for s in range(key_ref.shape[0]):
        out_ref[s] = key_ref[s].T


def attend_body(blocks, heads, *refs):
    pieces, (key_ref, value_ref, length_ref) = refs[:blocks], refs[blocks : blocks + 3]
    outs = refs[blocks + 3 : 2 * blocks + 3]
    row_ref, query_ref, mixed_ref = refs[2 * blocks + 3 :]
    me = lax.axis_index("yz")
    part = pieces[0].shape[1]
    seqs, head, slots = key_ref.shape
    scale = 1.0 / jnp.sqrt(jnp.float32(head))
    for j, piece in enumerate(pieces):
        row_ref[:, pl.ds(pl.multiple_of((me ^ j) * part, 128), part)] = piece[...].astype(jnp.float32)
    for h in range(heads):
        query_ref[h] = row_ref[:, h * head : (h + 1) * head]
    slot = lax.broadcasted_iota(jnp.int32, (1, slots), 1)
    width = heads * head
    queries = [query_ref[:, s, :] for s in range(seqs)]
    owns = [
        jnp.sum(queries[s] * row_ref[s : s + 1, width : width + head], axis=1, keepdims=True) * scale
        for s in range(seqs)
    ]
    scores = [
        lax.dot_general(
            queries[s].astype(jnp.bfloat16),
            key_ref[s],
            (((1,), (0,)), ((), ())),
            preferred_element_type=jnp.float32,
        )
        for s in range(seqs)
    ]
    masked = [jnp.where(slot < length_ref[s], scores[s] * scale, -jnp.inf) for s in range(seqs)]
    tops = [jnp.maximum(jnp.max(masked[s], axis=1, keepdims=True), owns[s]) for s in range(seqs)]
    weights = [jnp.exp(masked[s] - tops[s]) for s in range(seqs)]
    own_weights = [jnp.exp(owns[s] - tops[s]) for s in range(seqs)]
    totals = [jnp.sum(weights[s], axis=1, keepdims=True) + own_weights[s] for s in range(seqs)]
    probs = [(weights[s] / totals[s]).astype(jnp.bfloat16) for s in range(seqs)]
    mixed = [
        jnp.dot(probs[s], value_ref[s], preferred_element_type=jnp.float32) for s in range(seqs)
    ]
    for s in range(seqs):
        own_prob = (own_weights[s] / totals[s]).astype(jnp.bfloat16).astype(jnp.float32)
        value_new = row_ref[s : s + 1, width + head : width + 2 * head]
        mixed_ref[:, s, :] = mixed[s] + own_prob * value_new
    each = heads // blocks
    for j, out in enumerate(outs):
        first = (me ^ j) * each
        for h in range(each):
            out[:, h * head : (h + 1) * head] = mixed_ref[first + h].astype(jnp.bfloat16)


def attend(pieces, cache_keys, cache_values, cache_lengths, width):
    seqs, slots, head = cache_keys.shape
    blocks, heads = len(pieces), width // head
    keys = call(
        turn_body,
        struct((seqs, head, slots)),
        [VMEM],
        [near(cache_keys)],
        flops=seqs * slots * head,
        traffic=4 * seqs * slots * head,
    )
    values = pltpu.with_memory_space_constraint(cache_values, pltpu.VMEM)
    return call(
        functools.partial(attend_body, blocks, heads),
        [struct((seqs, width // blocks))] * blocks,
        [VMEM] * (blocks + 2) + [SMEM],
        [*pieces, keys, values, cache_lengths],
        order=B2,
        limit=12,
        scratch=[
            pltpu.VMEM((seqs, width + 2 * head), jnp.float32),
            pltpu.VMEM((heads, seqs, head), jnp.float32),
            pltpu.VMEM((heads, seqs, head), jnp.float32),
        ],
        flops=50_000_000_000,
        traffic=4 * seqs * slots * head,
    )


def cut_body(*refs):
    rows = jnp.concatenate([r[...] for r in refs[:4]], axis=0)
    whole, early, late = refs[4:]
    whole[...] = rows
    early[...] = rows[:, : early.shape[1]]
    late[...] = rows[:, early.shape[1] :]


def join_body(*refs):
    refs[-1][...] = jnp.concatenate([r[...] for r in refs[:-1]], axis=0)


def place_body(n, *refs):
    pieces, out_ref = refs[:n], refs[n]
    me = lax.axis_index("gx")
    total = pieces[0][...]
    for p in pieces[1:]:
        total = total + p[...].astype(jnp.float32)
    each = out_ref.shape[1]
    for k in range(out_ref.shape[0]):
        out_ref[me ^ k] = total[k * each : (k + 1) * each].astype(jnp.bfloat16)


def shards(tokens, gain, w_qkv, w_out, cache_keys, cache_values, cache_lengths):
    groups, blocks = lax.axis_size("gx"), lax.axis_size("yz")
    seqs, depth = tokens.shape[0], w_qkv.shape[0]
    width = w_out.shape[0] * blocks
    normed = call(
        norm_body,
        [struct((seqs, depth))] * groups,
        [ANY, ANY],
        [far(tokens), far(gain.reshape(1, -1))],
        scratch=[
            pltpu.VMEM(tokens.shape, tokens.dtype),
            pltpu.VMEM((1, gain.shape[0]), gain.dtype),
            pltpu.SemaphoreType.DMA((2,)),
        ],
        flops=50_000_000_000,
    )
    half = depth // 2
    mine, *halves = call(
        cut_body,
        [struct((groups * seqs, size)) for size in (depth, half, half)],
        [VMEM] * groups,
        exchange(normed, "gx"),
        order=A1,
    )
    one = swap(mine, "yz", 1)
    two = [swap(part, "yz", 2) for part in halves]
    three = [swap(part, "yz", 1) for part in two]
    own, one, two, three = dot([[mine], [one], two, three], w_qkv, kept=(0, 1, 2, 3), order=A2)
    two = call(add_body, struct(two.shape, WIDE), [VMEM] * 2, [two, swap(three, "gx", 1)])
    parts = call(
        total_body,
        [struct((seqs, w_qkv.shape[1]))] * blocks,
        [VMEM] * 3,
        [own, swap(two, "gx", 2), swap(one, "gx", 1)],
        order=B1,
    )
    attended = attend(exchange(parts, "yz"), cache_keys, cache_values, cache_lengths, width)
    got = exchange(attended, "yz")
    mine = call(join_body, struct((4 * seqs, got[0].shape[1])), [VMEM] * 4, got, flops=50_000_000_000, order=C1)
    two = swap(mine, "gx", 2)
    pieces = [[mine], [swap(mine, "gx", 1)], [two], [swap(two, "gx", 1)]]
    sums = exchange(dot(pieces, w_out, order=C2), "yz")
    return call(
        functools.partial(place_body, blocks),
        struct((groups, seqs, w_out.shape[1])),
        [VMEM] * blocks,
        sums,
        order=D,
    )


def attend_local(qkv, cache_keys, cache_values, cache_lengths, width):
    seq_rows = qkv.shape[0]
    head = cache_keys.shape[2]
    slots = cache_keys.shape[1]
    scale = 1.0 / jnp.sqrt(jnp.float32(head))
    query = qkv[:, :width].reshape(seq_rows, width // head, head)
    key_new = qkv[:, width : width + head]
    value_new = qkv[:, width + head :]
    scores = (
        jnp.einsum("shd,std->sht", query, cache_keys, preferred_element_type=jnp.float32) * scale
    )
    own = jnp.einsum("shd,sd->sh", query, key_new, preferred_element_type=jnp.float32) * scale
    valid = jnp.arange(slots, dtype=jnp.int32)[None, None, :] < cache_lengths[:, None, None]
    masked = jnp.where(valid, scores, -jnp.inf)
    top = jnp.maximum(jnp.max(masked, axis=2), own)
    weights = jnp.where(valid, jnp.exp(masked - top[:, :, None]), 0.0)
    own_weight = jnp.exp(own - top)
    total = jnp.sum(weights, axis=2) + own_weight
    probs = (weights / total[:, :, None]).astype(jnp.bfloat16)
    own_prob = (own_weight / total).astype(jnp.bfloat16)
    mixed = jnp.einsum("sht,std->shd", probs, cache_values, preferred_element_type=jnp.float32)
    mixed = (
        mixed + own_prob.astype(jnp.float32)[:, :, None] * value_new.astype(jnp.float32)[:, None, :]
    )
    return mixed.reshape(seq_rows, width).astype(jnp.bfloat16)


def shards_any(tokens, gain, w_qkv, w_out, cache_keys, cache_values, cache_lengths):
    seq_rows = tokens.shape[0]
    groups = lax.axis_size("gx")
    blocks = lax.axis_size("yz")
    width = w_out.shape[0] * blocks
    xf = tokens.astype(jnp.float32)
    mean = jnp.mean(xf, axis=1, keepdims=True)
    centered = xf - mean
    variance = jnp.mean(centered * centered, axis=1, keepdims=True)
    normed = (centered / jnp.sqrt(variance + 1e-05) * gain[None, :]).astype(jnp.bfloat16)
    feature_rows = lax.all_to_all(normed, "gx", split_axis=1, concat_axis=0, tiled=True)
    column_count = w_qkv.shape[1]
    partial_value = jnp.dot(
        lax.all_gather(feature_rows, "yz", axis=0, tiled=True),
        w_qkv,
        preferred_element_type=jnp.float32,
    )
    partial_value = partial_value.reshape(blocks, groups, seq_rows, column_count)
    summed = lax.psum_scatter(partial_value, "gx", scatter_dimension=1, tiled=True)
    summed = summed.reshape(blocks, seq_rows, column_count).astype(jnp.bfloat16)
    received = lax.all_to_all(summed, "yz", split_axis=0, concat_axis=0, tiled=True)
    qkv = received.transpose(1, 0, 2).reshape(seq_rows, blocks * column_count)
    attended = attend_local(qkv, cache_keys, cache_values, cache_lengths, width)
    feature_block = w_out.shape[0]
    split = attended.reshape(seq_rows, blocks, feature_block)
    received = lax.all_to_all(split, "yz", split_axis=1, concat_axis=0, tiled=True)
    received = received.reshape(blocks * seq_rows, feature_block)
    everyone = lax.all_gather(received, "gx", axis=0, tiled=True)
    everyone = everyone.reshape(groups, blocks * seq_rows, feature_block)
    summed = lax.psum_scatter(
        jnp.einsum("gcf,fd->cgd", everyone, w_out, preferred_element_type=jnp.float32),
        "yz",
        scatter_dimension=0,
        tiled=True,
    )
    return summed.transpose(1, 0, 2).astype(jnp.bfloat16)


def solution(mesh):
    placed = (
        P(("parts", "gx", "yz"), None),
        P(),
        P("gx", "yz"),
        P("yz", "gx"),
        P(("parts", "gx", "yz"), None, None),
        P(("parts", "gx", "yz"), None, None),
        P(("parts", "gx", "yz")),
    )
    small = mesh.shape["gx"] == 4 and mesh.shape["yz"] == 4
    return jax.shard_map(
        shards if small else shards_any,
        mesh=mesh,
        in_specs=placed,
        out_specs=P(None, ("parts", "yz"), "gx"),
        check_vma=False,
    )
```
